128 devices in a mesh: gx: 16 (over x_hi, y, core), gy: 8 (over x_lo, z).
Axes of the slice: x: 4 (x_hi: 2, x_lo: 2; x = x_hi * 2 + x_lo), y: 4, z: 4, core: 2. Of those that a mesh axis runs over, the one named last changes fastest.
Arguments:
- positions: float32 [3, 64, 32, 4, 128], P(None, 'gx', 'gy'), may hold values from 0 to 128, as said below
- velocity: float32 [3, 64, 32, 4, 128], P(None, 'gx', 'gy'), may hold values from -5 to 5
- density: float32 [64, 32, 4, 128], P('gx', 'gy'), may hold values from 0.98 to 1.02
- masses: float32 [64, 32, 4, 128], P('gx', 'gy'), may hold values from 0.04 to 0.08
- counts: int32 [64, 32, 4], P('gx', 'gy'), may hold values from 0 to 128, as said below
Outputs:
- density_rate: float32 [64, 32, 4, 128], P('gx', 'gy')
- acceleration: float32 [3, 64, 32, 4, 128], P(None, 'gx', 'gy')
The draws below stay inside these ranges and needn't reach their ends.
Inputs may be any that keep to these rules, and one draw needn't show every extreme that they name: `positions`: the particle in a slot of the block at indices (a, b, c) lies in the cell [2a, 2a + 2) x [2b, 2b + 2) x [2c, 2c + 2); values in slots that are not live are meaningless. `counts`: slots below a block's count are live. The bottom block of every column inside the water column is full.
All inputs are finite; a program needn't handle non-finite values.
Results may differ from the reference program's by a relative error of at most 0.0001.
Values sent between devices are 32-bit elements; how exact they have to be, the bound alone decides.
No kernel may reach another device: no remote copies, remote signals or barrier semaphores. Data moves between devices by JAX's collectives and lax.ppermute only.
A program may use at most 64 MiB of HBM per device.

```python
import math
import jax
import jax.numpy as jnp
import numpy as np
from jax import lax

SLOTS = 128
BZ = 4
NBX = 64
NBY = 32


def draw_positions(key, part):
    shape = (3, NBX, NBY, BZ, SLOTS)
    inside = jax.random.uniform(key, shape, jnp.float32)
    cells = jnp.stack([lax.broadcasted_iota(jnp.float32, shape[1:], 0), lax.broadcasted_iota(jnp.float32, shape[1:], 1), lax.broadcasted_iota(jnp.float32, shape[1:], 2)], 0)
    return 2.0 * (cells + inside)


def draw_counts(key, part):
    shape = (NBX, NBY, BZ)
    key_full, key_floor, key_upper = jax.random.split(key, 3)
    column = lax.broadcasted_iota(jnp.int32, shape, 0)
    level = lax.broadcasted_iota(jnp.int32, shape, 2)
    in_dam = column < max(1, NBX // 2)
    water_top = max(1, 7 * BZ // 8)
    full_part = jax.random.randint(key_full, shape, 96, 129)
    floor_part = jax.random.randint(key_floor, shape, 32, 129)
    upper_part = jax.random.randint(key_upper, shape, 0, 65)
    dam_counts = jnp.where(level == 0, 128, jnp.where(level < water_top, full_part, 0))
    flat_counts = jnp.where(level == 0, floor_part, jnp.where(level == 1, upper_part, 0))
    return jnp.where(in_dam, dam_counts, flat_counts).astype(jnp.int32)


def levels(stream_key, shape, cuts, low, high):
    def one(dim, shards_of):
        heights = jax.random.uniform(jax.random.fold_in(jax.random.fold_in(stream_key, 6), dim), (shards_of,), jnp.float32, low / len(cuts), high / len(cuts))
        return jnp.repeat(jnp.exp(heights), shape[dim] // shards_of).reshape((-1,) + (1,) * (len(shape) - dim - 1))

    factor_of = one(*cuts[0])
    for cut in cuts[1:]:
        factor_of = factor_of * one(*cut)
    return factor_of


def gaussian(rng, dims, scale, limit, shards=(), dtype=jnp.bfloat16):
    values = scale * jax.random.normal(rng, dims, jnp.float32)
    if shards:
        values = values * levels(rng, dims, shards, -0.22, 0.18)
    return jnp.clip(values, -limit, limit).astype(dtype)


def setup_inputs(seed: int = 0) -> dict:
    arg_keys = jax.random.split(jax.random.key(seed), 6)
    return {
        "positions": draw_positions(jax.random.fold_in(arg_keys[5], 71), 0),
        "velocity": gaussian(arg_keys[1], (3, NBX, NBY, BZ, SLOTS), 1.0, 5.0, ((1, 16), (2, 8)), jnp.float32),
        "density": jnp.clip(0.98 + 0.03999996 * jax.random.uniform(arg_keys[2], (NBX, NBY, BZ, SLOTS), jnp.float32) ** levels(arg_keys[2], (NBX, NBY, BZ, SLOTS), ((0, 16), (1, 8)), -0.2, 0.2), 0.98, 1.02),
        "masses": jnp.clip(jnp.exp(math.log(0.08) - 0.6931472 * jax.random.uniform(arg_keys[3], (NBX, NBY, BZ, SLOTS), jnp.float32) ** levels(arg_keys[3], (NBX, NBY, BZ, SLOTS), ((0, 16), (1, 8)), -0.2, 0.2)), 0.04, 0.08),
        "counts": draw_counts(jax.random.fold_in(arg_keys[5], 71), 0),
    }


KERNEL_GRAD = 105.0 / (16.0 * math.pi)
REGULAR = 0.2
STIFFNESS = 100.0 / 7.0
VISCOUS = 0.5
GRAVITY = 1.0
SOFTEN = 0.01
SYM_PAIRS = ((0, 0), (1, 1), (2, 2), (0, 1), (0, 2), (1, 2))
SYM_INDEX = ((0, 3, 4), (3, 1, 5), (4, 5, 2))
FULL_OFFSETS = tuple([(0, 0, 0)] + [(a, b, c) for a in (-1, 0, 1) for b in (-1, 0, 1) for c in (-1, 0, 1) if (a, b, c) != (0, 0, 0)])

def neighbour_tables(local_shape, ext_shape, anchor, offsets):
    width_x, width_y, height = local_shape
    ext_x, ext_y, ext_z = ext_shape
    target_list = []
    partner_list = []
    for a in range(width_x):
        for b in range(width_y):
            for c in range(height):
                pos_a = a + anchor[0]
                pos_b = b + anchor[1]
                pos_c = c + anchor[2]
                target_list.append((pos_a * ext_y + pos_b) * ext_z + pos_c)
                partner_list.append([((pos_a + d[0]) * ext_y + pos_b + d[1]) * ext_z + pos_c + d[2] for d in offsets])
    return (jnp.asarray(np.array(target_list, np.int32)), jnp.asarray(np.array(partner_list, np.int32)))

def build_state(positions, velocity, density, masses, live_mask):
    press_term = STIFFNESS * (density ** 7 - 1.0) / (density * density)
    return jnp.concatenate([positions, velocity, (masses * live_mask)[None], (live_mask * masses / density)[None], density[None], press_term[None]], 0)

def kernel_terms(target, partner):
    delta = target[0:3][None, :, :, None] - partner[:, 0:3][:, :, None, :]
    radius_sq = lax.optimization_barrier(jnp.sum(delta * delta, axis=1))
    falloff = jnp.maximum(1.0 - 0.5 * jnp.sqrt(radius_sq), 0.0)
    return (delta, radius_sq, KERNEL_GRAD * falloff * falloff * falloff)

def tensor_pair(target, partner):
    delta, radius_sq, kernel_c = kernel_terms(target, partner)
    weight_i = kernel_c * partner[:, 7][:, None, :]
    weight_j = kernel_c * target[7][None, :, None]
    side_i = []
    side_j = []
    for pair_ab in SYM_PAIRS:
        outer = delta[:, pair_ab[0]] * delta[:, pair_ab[1]]
        side_i.append(lax.optimization_barrier(jnp.sum(weight_i * outer, axis=(0, 2))))
        side_j.append(lax.optimization_barrier(jnp.sum(weight_j * outer, axis=1)))
    return (jnp.stack(side_i, 0), jnp.stack(side_j, 1))

def motion_pair(target, target_corr, partner, partner_corr):
    delta, radius_sq, kernel_c = kernel_terms(target, partner)
    grads = []
    for a in range(3):
        along_i = target_corr[SYM_INDEX[a][0]][None, :, None] * delta[:, 0]
        along_j = partner_corr[:, SYM_INDEX[a][0]][:, None, :] * delta[:, 0]
        for b in (1, 2):
            along_i = along_i + target_corr[SYM_INDEX[a][b]][None, :, None] * delta[:, b]
            along_j = along_j + partner_corr[:, SYM_INDEX[a][b]][:, None, :] * delta[:, b]
        grads.append(-0.5 * kernel_c * (along_i + along_j))
    vel_diff = target[3:6][None, :, :, None] - partner[:, 3:6][:, :, None, :]
    v_dot_g = vel_diff[:, 0] * grads[0] + vel_diff[:, 1] * grads[1] + vel_diff[:, 2] * grads[2]
    v_dot_x = vel_diff[:, 0] * delta[:, 0] + vel_diff[:, 1] * delta[:, 1] + vel_diff[:, 2] * delta[:, 2]
    mean_rho = 0.5 * (target[8][None, :, None] + partner[:, 8][:, None, :])
    viscous = -VISCOUS * jnp.minimum(v_dot_x, 0.0) / (radius_sq + SOFTEN) / mean_rho
    pressure = target[9][None, :, None] + partner[:, 9][:, None, :] + viscous
    mass_j = partner[:, 6][:, None, :]
    mass_i = target[6][None, :, None]
    side_i = [lax.optimization_barrier(jnp.sum(mass_j * v_dot_g, axis=(0, 2)))]
    side_j = [lax.optimization_barrier(jnp.sum(mass_i * v_dot_g, axis=1))]
    for a in range(3):
        side_i.append(-lax.optimization_barrier(jnp.sum(mass_j * pressure * grads[a], axis=(0, 2))))
        side_j.append(lax.optimization_barrier(jnp.sum(mass_i * pressure * grads[a], axis=1)))
    return (jnp.stack(side_i, 0), jnp.stack(side_j, 1))

def invert_blocks(moment):
    a = moment[..., 0, :] + REGULAR
    d = moment[..., 1, :] + REGULAR
    f = moment[..., 2, :] + REGULAR
    b = moment[..., 3, :]
    c = moment[..., 4, :]
    e = moment[..., 5, :]
    cof_xx = d * f - e * e
    cof_xy = c * e - b * f
    cof_xz = b * e - c * d
    cof_yy = a * f - c * c
    cof_yz = b * c - a * e
    cof_zz = a * d - b * b
    determinant = a * cof_xx + b * cof_xy + c * cof_xz
    return jnp.stack([cof_xx, cof_yy, cof_zz, cof_xy, cof_xz, cof_yz], -2) / determinant[..., None, :]

def reference(positions, velocity, density, masses, counts):
    width_x, width_y, height, slot_count = density.shape
    live_mask = (lax.broadcasted_iota(jnp.int32, density.shape, 3) < counts[..., None]).astype(jnp.float32)
    blocks = jnp.transpose(build_state(positions, velocity, density, masses, live_mask), (1, 2, 3, 0, 4))
    spread = ((1, 1), (1, 1), (1, 1), (0, 0), (0, 0))
    flat_state = jnp.pad(blocks, spread).reshape(-1, 10, slot_count)
    targets, partners = neighbour_tables((width_x, width_y, height), (width_x + 2, width_y + 2, height + 2), (1, 1, 1), FULL_OFFSETS)

    def first_pass(block_item):
        own_side, far_side = tensor_pair(flat_state[block_item[0]], flat_state[block_item[1]])
        return own_side
    moment = lax.map(first_pass, (targets, partners))
    correction = invert_blocks(moment).reshape(width_x, width_y, height, 6, slot_count)
    flat_corr = jnp.pad(correction, spread).reshape(-1, 6, slot_count)

    def second_pass(block_item):
        own_side, far_side = motion_pair(flat_state[block_item[0]], flat_corr[block_item[0]], flat_state[block_item[1]], flat_corr[block_item[1]])
        return own_side
    rates = lax.map(second_pass, (targets, partners)).reshape(width_x, width_y, height, 4, slot_count)
    density_rate = rates[..., 0, :] * live_mask
    acceleration = jnp.transpose(rates[..., 1:4, :], (3, 0, 1, 2, 4)) * live_mask[None]
    acceleration = acceleration.at[2].add(-GRAVITY * live_mask)
    return (density_rate, acceleration)
```

```python
import functools
import math

import jax
import jax.numpy as jnp
import numpy as np
from jax import lax
from jax.experimental import pallas as pl
from jax.experimental.pallas import tpu as pltpu
from jax.sharding import PartitionSpec as P

KERNEL_GRAD = 105.0 / (16.0 * math.pi)
REGULAR = 0.2
STIFFNESS = 100.0 / 7.0
GRAVITY = 1.0
SOFTEN = 0.01
TINY = 1e-12
SYM_PAIRS = ((0, 0), (1, 1), (2, 2), (0, 1), (0, 2), (1, 2))
SYM_INDEX = ((0, 3, 4), (3, 1, 5), (4, 5, 2))
F32 = jnp.float32
BF16 = jnp.bfloat16
LOCAL = 64
TOTAL = 144
KA = 80
M1 = 32
M2 = 128
MW = 48
NB = 9
W_ROWS = 40
LEVEL_PAIRS = ((0, 0), (0, 1), (1, 0), (1, 1), (1, 2), (2, 1), (2, 2), (2, 3), (3, 2), (3, 3))


def column_bases():
    base = np.zeros((6, 6), np.int32)
    for a in range(6):
        for b in range(6):
            if a == 0:
                base[a, b] = 96 + b * 4
            elif a == 5:
                base[a, b] = 120 + b * 4
            elif b == 0:
                base[a, b] = 64 + (a - 1) * 4
            elif b == 5:
                base[a, b] = 80 + (a - 1) * 4
            else:
                base[a, b] = ((a - 1) * 4 + (b - 1)) * 4
    return base


def item_table(columns):
    base = column_bases()
    rows = []
    for c, d in LEVEL_PAIRS:
        for a, b in columns:
            row = [((a - 1) * 4 + (b - 1)) * 4 + c]
            for da in (-1, 0, 1):
                for db in (-1, 0, 1):
                    row.append(base[a + da, b + db] + d)
            rows.append(row)
    return np.asarray(rows, np.int32).reshape(-1)


def split3(x):
    h = x.astype(BF16).astype(F32)
    r = x - h
    m = r.astype(BF16).astype(F32)
    return h, m, r - m


def pair_rows(state, corner, k, with_targets, rows_ref, a_ref, b_ref, rho_ref):
    blk = pl.ds(pl.multiple_of(k * 8, 8), 8)
    x = [state[d, blk, :] - corner[d] for d in range(3)]
    v = [state[3 + d, blk, :] for d in range(3)]
    rho = state[6, blk, :]
    n2 = x[0] * x[0] + x[1] * x[1] + x[2] * x[2]
    xv = x[0] * v[0] + x[1] * v[1] + x[2] * v[2]
    one = jnp.ones_like(n2)
    zero = jnp.zeros_like(n2)
    xs = [split3(t) for t in x]
    vs = [split3(t) for t in v]
    rs = split3(rho)
    n2s = split3(n2)
    xvs = split3(xv)

    def put(group, parts):
        for r, p in enumerate(parts):
            rows_ref[pl.ds((group * 8 + r) * 8, 8), :] = p

    def get(group, b):
        return rows_ref[pl.ds(group * 64 + b, 8, stride=8), :]

    for s in range(3):
        put(s, [xs[d][s] for d in range(3)] + [vs[d][s] for d in range(3)] + [rs[s], one])
    put(3, list(n2s) + list(xvs) + [one, one])
    if with_targets:
        for s in range(3):
            put(4 + s, [-0.5 * xs[d][s] for d in range(3)] + [zero] * 5)
            put(7 + s, [-vs[d][s] for d in range(3)] + [-xs[d][s] for d in range(3)] + [zero] * 2)
        quarter = one * 0.25
        put(10, [-0.5 * xs[d][0] for d in range(3)] + [zero] * 4 + [0.25 * n2s[2]])
        put(11, [-vs[d][0] for d in range(3)] + [-xs[d][0] for d in range(3)] + [zero, xvs[2]])
        put(12, [quarter] * 3 + [zero] * 3 + [0.25 * n2s[0], 0.25 * n2s[1]])
        put(13, [zero] * 3 + [one] * 3 + [xvs[0], xvs[1]])
    pad = jnp.zeros((128 - KA, 128), F32)
    for b in range(8):
        g = [get(s, b) for s in range(4)]
        rows = jnp.concatenate([g[0]] * 3 + [g[1]] * 3 + [g[2]] * 3 + [g[3], pad], 0)
        cols = rows.T
        a_ref[k * 8 + b] = cols[:, :KA].astype(BF16)
        if rho_ref is not None:
            col = cols[:, 6:7] + cols[:, 30:31] + cols[:, 54:55]
            rho_ref[k * 8 + b] = jnp.broadcast_to(col, (128, 128))
        if with_targets:
            r2_rows = [get(10, b), get(5, b), get(6, b)] + [get(4 + s, b) for s in range(3)] * 2
            b_ref[k * 8 + b, :, :128] = jnp.concatenate(r2_rows + [get(12, b)], 0).astype(BF16)
            if rho_ref is not None:
                vx_rows = [get(11, b), get(8, b), get(9, b)] + [get(7 + s, b) for s in range(3)] * 2
                b_ref[k * 8 + b, :, 128:] = jnp.concatenate(vx_rows + [get(13, b)], 0).astype(BF16)


def store_features(rows_ref, out_ref, k, features, rows, first):
    at = first
    for f in features:
        for piece in split3(f):
            rows_ref[pl.ds(at * 8, 8), :] = piece
            at += 1
    return at


def gather_features(rows_ref, out_ref, k, rows):
    for b in range(8):
        out_ref[k * 8 + b] = rows_ref[pl.ds(b, rows, stride=8), :].astype(BF16)


def hi_lo(x):
    hi = x.astype(BF16)
    return hi, (x - hi.astype(F32)).astype(BF16)


def falloff_cubed(s2):
    q = jnp.maximum(1.0 - s2 * lax.rsqrt(s2), 0.0)
    return q * q * q


def pipeline(n, one, two, three):
    one(0, 0)
    one(1, 1)
    two(0, 0)

    def step(s, carry):
        t = 2 * s
        last = n - 1
        three(t, 0)
        two(t + 1, 1)
        one(jnp.minimum(t + 2, last), 0)
        three(t + 1, 1)
        two(jnp.minimum(t + 2, last), 0)
        one(jnp.minimum(t + 3, last), 1)
        return carry

    lax.fori_loop(0, n // 2, step, 0)


def moment_kernel(n_ref, tab, corner_ref, state, corr, a_ref, b_ref, f_ref, rows_ref, r_ref, c_ref, acc, sums):
    corner = [corner_ref[d] for d in range(3)]
    n = n_ref[0]

    def prepare(k, with_targets):
        pair_rows(state, corner, k, with_targets, rows_ref, a_ref, b_ref, None)
        blk = pl.ds(pl.multiple_of(k * 8, 8), 8)
        x = [state[d, blk, :] - corner[d] for d in range(3)]
        vol = state[7, blk, :] / state[6, blk, :]
        vx = [vol * t for t in x]
        features = [vol] + vx + [vx[p] * x[q] for p, q in SYM_PAIRS]
        at = store_features(rows_ref, f_ref, k, features, M1, 0)
        for r in range(at, M1):
            rows_ref[pl.ds(r * 8, 8), :] = jnp.zeros((8, 128), F32)
        gather_features(rows_ref, f_ref, k, M1)

    def first(k, carry):
        prepare(k, True)
        return carry

    def rest(k, carry):
        prepare(k, False)
        return carry

    lax.fori_loop(0, LOCAL // 8, first, 0)
    lax.fori_loop(LOCAL // 8, TOTAL // 8, rest, 0)
    acc[...] = jnp.zeros_like(acc)

    def one(t, p):
        i = tab[t * 10]
        lhs = jnp.concatenate([a_ref[tab[t * 10 + 1 + e]] for e in range(NB)], 0)
        r_ref[p] = jnp.dot(lhs, b_ref[i], preferred_element_type=F32)

    def two(t, p):
        for e in range(NB):
            rows = pl.ds(e * 128, 128)
            c = falloff_cubed(jnp.maximum(r_ref[p, rows, :], TINY))
            hi, lo = hi_lo(c)
            c_ref[p, rows, :128] = hi
            c_ref[p, rows, 128:] = lo

    def three(t, p):
        i = tab[t * 10]
        lhs = jnp.concatenate([f_ref[tab[t * 10 + 1 + e]] for e in range(NB)], 1)
        acc[i] += jnp.dot(lhs, c_ref[p], preferred_element_type=F32)

    pipeline(n, one, two, three)

    def collect(i, carry):
        both = acc[i, :, :128] + acc[i, :, 128:]
        sums[pl.ds(i, M1, stride=LOCAL), :] = both
        return carry

    lax.fori_loop(0, LOCAL, collect, 0)

    def finish(k, carry):
        blk = pl.ds(pl.multiple_of(k * 8, 8), 8)
        x = [state[d, blk, :] - corner[d] for d in range(3)]

        def total(f):
            at = [sums[pl.ds(pl.multiple_of((3 * f + s) * LOCAL + k * 8, 8), 8), :] for s in range(3)]
            return at[0] + (at[1] + at[2])

        t0 = total(0)
        t1 = [total(1 + d) for d in range(3)]
        mom = []
        for e, (p, q) in enumerate(SYM_PAIRS):
            value = (x[p] * t0 - t1[p]) * x[q] + (total(4 + e) - x[p] * t1[q])
            mom.append(KERNEL_GRAD * value)
        a, d, f = (mom[e] + REGULAR for e in range(3))
        b, c, e = mom[3:]
        cof_xx = d * f - e * e
        cof_xy = c * e - b * f
        cof_xz = b * e - c * d
        cof_yy = a * f - c * c
        cof_yz = b * c - a * e
        cof_zz = a * d - b * b
        scale = 1.0 / (a * cof_xx + b * cof_xy + c * cof_xz)
        for r, cof in enumerate((cof_xx, cof_yy, cof_zz, cof_xy, cof_xz, cof_yz)):
            corr[r, blk, :] = cof * scale
        return carry

    lax.fori_loop(0, LOCAL // 8, finish, 0)


def rate_kernel(n_ref, tab, corner_ref, state, corr, rate, a_ref, b_ref, rho_ref, f_ref, rows_ref, r_ref, c_ref, w_ref,
                acc, accw, sums, sumsw):
    corner = [corner_ref[d] for d in range(3)]
    n = n_ref[0]

    def pressure(rho):
        r2 = rho * rho
        return STIFFNESS * (r2 * r2 * r2 * rho - 1.0) / r2

    def times(sym, vec):
        return [sym[SYM_INDEX[p][0]] * vec[0] + sym[SYM_INDEX[p][1]] * vec[1] + sym[SYM_INDEX[p][2]] * vec[2]
                for p in range(3)]

    def prepare(k, with_targets):
        pair_rows(state, corner, k, with_targets, rows_ref, a_ref, b_ref, rho_ref)
        blk = pl.ds(pl.multiple_of(k * 8, 8), 8)
        x = [state[d, blk, :] - corner[d] for d in range(3)]
        v = [state[3 + d, blk, :] for d in range(3)]
        rho = state[6, blk, :]
        m = state[7, blk, :]
        sym = [corr[r, blk, :] for r in range(6)]
        m_sym = [m * t for t in sym]
        m_sym_x = times(m_sym, x)
        m_sym_v = times(m_sym, v)
        prs = pressure(rho)
        mp = m * prs
        mv = [m * t for t in v]
        shared = [m] + [m * t for t in x] + m_sym + m_sym_x
        own = (mv + [mv[p] * x[q] for p in range(3) for q in range(3)] + m_sym_v
               + [v[0] * m_sym_x[0] + v[1] * m_sym_x[1] + v[2] * m_sym_x[2]]
               + [mp] + [mp * t for t in x] + [prs * t for t in m_sym] + [prs * t for t in m_sym_x])
        at = store_features(rows_ref, f_ref, k, shared, M2, 0)
        for r in range(at, W_ROWS):
            rows_ref[pl.ds(r * 8, 8), :] = jnp.zeros((8, 128), F32)
        at = store_features(rows_ref, f_ref, k, own, M2, W_ROWS)
        for r in range(at, M2):
            rows_ref[pl.ds(r * 8, 8), :] = jnp.zeros((8, 128), F32)
        gather_features(rows_ref, f_ref, k, M2)

    def first(k, carry):
        prepare(k, True)
        return carry

    def rest(k, carry):
        prepare(k, False)
        return carry

    lax.fori_loop(0, LOCAL // 8, first, 0)
    lax.fori_loop(LOCAL // 8, TOTAL // 8, rest, 0)
    acc[...] = jnp.zeros_like(acc)
    accw[...] = jnp.zeros_like(accw)

    def one(t, p):
        i = tab[t * 10]
        lhs = jnp.concatenate([a_ref[tab[t * 10 + 1 + e]] for e in range(NB)], 0)
        r_ref[p] = jnp.dot(lhs, b_ref[i], preferred_element_type=F32)

    def two(t, p):
        i = tab[t * 10]
        k8 = pl.multiple_of((i // 8) * 8, 8)
        rho_i = state[6, pl.ds(i, 1), :]
        for e in range(NB):
            j = tab[t * 10 + 1 + e]
            rows = pl.ds(e * 128, 128)
            s2 = jnp.maximum(r_ref[p, rows, :128], TINY)
            c = falloff_cubed(s2)
            hi, lo = hi_lo(c)
            c_ref[p, rows, :128] = hi
            c_ref[p, rows, 128:] = lo
            bottom = (s2 + 0.25 * SOFTEN) * (rho_ref[j] + rho_i)
            w = c * jnp.minimum(r_ref[p, rows, 128:], 0.0) * pltpu.reciprocal(bottom)
            hi, lo = hi_lo(w)
            w_ref[p, rows, :128] = hi
            w_ref[p, rows, 128:] = lo

    def three(t, p):
        i = tab[t * 10]
        lhs = jnp.concatenate([f_ref[tab[t * 10 + 1 + e]] for e in range(NB)], 1)
        acc[i] += jnp.dot(lhs, c_ref[p], preferred_element_type=F32)
        accw[i] += jnp.dot(lhs[:MW], w_ref[p], preferred_element_type=F32)

    pipeline(n, one, two, three)

    def collect(i, carry):
        sums[pl.ds(i, M2, stride=LOCAL), :] = acc[i, :, :128] + acc[i, :, 128:]
        sumsw[pl.ds(i, MW, stride=LOCAL), :] = accw[i, :, :128] + accw[i, :, 128:]
        return carry

    lax.fori_loop(0, LOCAL, collect, 0)

    def finish(k, carry):
        blk = pl.ds(pl.multiple_of(k * 8, 8), 8)
        x = [state[d, blk, :] - corner[d] for d in range(3)]
        v = [state[3 + d, blk, :] for d in range(3)]
        prs = pressure(state[6, blk, :])
        sym = [corr[r, blk, :] for r in range(6)]

        def total(ref, first_row, f):
            at = [ref[pl.ds(pl.multiple_of((first_row + 3 * f + s) * LOCAL + k * 8, 8), 8), :] for s in range(3)]
            return at[0] + (at[1] + at[2])

        shared = [total(sums, 0, f) for f in range(13)]
        own = [total(sums, W_ROWS, f) for f in range(29)]
        visc = [total(sumsw, 0, f) for f in range(13)]
        m0, mx, mk, mkx = shared[0], shared[1:4], shared[4:10], shared[10:13]
        mv, mvx, mkv, mvkx = own[0:3], own[3:12], own[12:15], own[15]
        p0, px, pk, pkx = own[16], own[17:20], own[20:26], own[26:29]
        w0, wx, wk, wkx = visc[0], visc[1:4], visc[4:10], visc[10:13]
        vx = [[v[p] * (x[q] * m0 - mx[q]) - (mv[p] * x[q] - mvx[3 * p + q]) for q in range(3)] for p in range(3)]
        inner = jnp.zeros_like(m0)
        for p in range(3):
            for q in range(3):
                inner = inner + sym[SYM_INDEX[p][q]] * vx[p][q]
        mk_x = times(mk, x)
        for p in range(3):
            inner = inner + v[p] * (mk_x[p] - mkx[p]) - x[p] * mkv[p]
        inner = inner + mvkx
        rate[0, blk, :] = (-0.5 * KERNEL_GRAD) * inner
        near = [prs * (x[p] * m0 - mx[p]) + (x[p] * p0 - px[p]) - 0.25 * (x[p] * w0 - wx[p]) for p in range(3)]
        mine = times(sym, near)
        pk_x = times(pk, x)
        wk_x = times(wk, x)
        for p in range(3):
            far = prs * (mk_x[p] - mkx[p]) + (pk_x[p] - pkx[p]) - 0.25 * (wk_x[p] - wkx[p])
            rate[1 + p, blk, :] = (0.5 * KERNEL_GRAD) * (mine[p] + far)
        return carry

    lax.fori_loop(0, LOCAL // 8, finish, 0)


VMEM = pl.BlockSpec(memory_space=pltpu.VMEM)
SMEM = pl.BlockSpec(memory_space=pltpu.SMEM)
ALL_COLUMNS = tuple((a, b) for a in range(1, 5) for b in range(1, 5))


def run_moments(n, table, corner, state):
    return pl.pallas_call(
        moment_kernel,
        out_shape=jax.ShapeDtypeStruct((6, LOCAL, 128), F32),
        in_specs=[SMEM, SMEM, SMEM, VMEM],
        out_specs=VMEM,
        scratch_shapes=[
            pltpu.VMEM((TOTAL, 128, KA), BF16),
            pltpu.VMEM((LOCAL, KA, 128), BF16),
            pltpu.VMEM((TOTAL, M1, 128), BF16),
            pltpu.VMEM((14 * 64, 128), F32),
            pltpu.VMEM((2, NB * 128, 128), F32),
            pltpu.VMEM((2, NB * 128, 256), BF16),
            pltpu.VMEM((LOCAL, M1, 256), F32),
            pltpu.VMEM((M1 * LOCAL, 128), F32),
        ],
        compiler_params=pltpu.CompilerParams(vmem_limit_bytes=56 * 2**20),
        name="moments",
    )(n, table, corner, state)


def run_rates(n, table, corner, state, corr):
    return pl.pallas_call(
        rate_kernel,
        out_shape=jax.ShapeDtypeStruct((4, LOCAL, 128), F32),
        in_specs=[SMEM, SMEM, SMEM, VMEM, VMEM],
        out_specs=VMEM,
        scratch_shapes=[
            pltpu.VMEM((TOTAL, 128, KA), BF16),
            pltpu.VMEM((LOCAL, KA, 256), BF16),
            pltpu.VMEM((TOTAL, 128, 128), F32),
            pltpu.VMEM((TOTAL, M2, 128), BF16),
            pltpu.VMEM((M2 * 8, 128), F32),
            pltpu.VMEM((2, NB * 128, 256), F32),
            pltpu.VMEM((2, NB * 128, 256), BF16),
            pltpu.VMEM((2, NB * 128, 256), BF16),
            pltpu.VMEM((LOCAL, M2, 256), F32),
            pltpu.VMEM((LOCAL, MW, 256), F32),
            pltpu.VMEM((M2 * LOCAL, 128), F32),
            pltpu.VMEM((MW * LOCAL, 128), F32),
        ],
        compiler_params=pltpu.CompilerParams(vmem_limit_bytes=60 * 2**20),
        name="rates",
    )(n, table, corner, state, corr)


def shifted(value, axis, steps):
    count = lax.axis_size(axis)
    first, last = (max(0, -steps), min(count, count - steps))
    return lax.ppermute(value, axis, [(source, source + steps) for source in range(first, last)])


def with_halo(blocks):
    ch = blocks.shape[0]
    low_y = shifted(blocks[:, :, -1:], "gy", 1)
    high_y = shifted(blocks[:, :, :1], "gy", -1)

    def row(a):
        return jnp.concatenate([low_y[:, a:a + 1], blocks[:, a:a + 1], high_y[:, a:a + 1]], 2)

    low_x = shifted(row(3), "gx", 1)
    high_x = shifted(row(0), "gx", -1)
    return jnp.concatenate([t.reshape(ch, -1, 128) for t in (blocks, low_y, high_y, low_x, high_x)], 1)


def occupied_levels(mass):
    any_live = jnp.max(mass.reshape(TOTAL // 4, 4, 128), axis=(0, 2)) > 0.0
    return jnp.max(jnp.where(any_live, jnp.arange(1, 5, dtype=jnp.int32), 1))


def body(positions, velocity, density, masses, counts):
    shape = density.shape
    live = lax.broadcasted_iota(jnp.int32, shape, 3) < counts[..., None]
    blocks = jnp.concatenate(
        [
            jnp.where(live, positions, 0.0),
            jnp.where(live, velocity, 0.0),
            jnp.where(live, density, 1.0)[None],
            jnp.where(live, masses, 0.0)[None],
        ],
        0,
    )
    state = with_halo(blocks)
    state = state.at[6].set(jnp.where(state[6] > 0.0, state[6], 1.0))
    centre_x = (lax.axis_index("gx") * 8 + 4).astype(F32)
    centre_y = (lax.axis_index("gy") * 8 + 4).astype(F32)
    corner = jnp.stack([centre_x, centre_y, jnp.float32(4.0)])
    table = jnp.asarray(item_table(ALL_COLUMNS))
    n = ((3 * occupied_levels(state[7]) - 2) * 16).reshape(1)
    corr = run_moments(n, table, corner, state)
    corr_all = with_halo(corr.reshape((6,) + shape))
    rates = run_rates(n, table, corner, state, corr_all).reshape((4,) + shape)
    density_rate = jnp.where(live, rates[0], 0.0)
    pull = jnp.asarray([0.0, 0.0, -GRAVITY], F32).reshape(3, 1, 1, 1, 1)
    acceleration = jnp.where(live, rates[1:4] + pull, 0.0)
    return (density_rate, acceleration)


def solution(mesh):
    return jax.shard_map(
        body,
        mesh=mesh,
        in_specs=(
            P(None, "gx", "gy", None, None),
            P(None, "gx", "gy", None, None),
            P("gx", "gy", None, None),
            P("gx", "gy", None, None),
            P("gx", "gy", None),
        ),
        out_specs=(P("gx", "gy", None, None), P(None, "gx", "gy", None, None)),
        check_vma=False,
    )
```

```python
import functools
import math

import jax
import jax.numpy as jnp
import numpy as np
from jax import lax
from jax.experimental import pallas as pl
from jax.experimental.pallas import tpu as pltpu
from jax.sharding import PartitionSpec as P

KERNEL_GRAD = 105.0 / (16.0 * math.pi)
REGULAR = 0.2
STIFFNESS = 100.0 / 7.0
GRAVITY = 1.0
SOFTEN = 0.01
TINY = 1e-12
SYM_PAIRS = ((0, 0), (1, 1), (2, 2), (0, 1), (0, 2), (1, 2))
SYM_INDEX = ((0, 3, 4), (3, 1, 5), (4, 5, 2))
F32 = jnp.float32
BF16 = jnp.bfloat16
LOCAL = 64
TOTAL = 144
KA = 80
M1 = 32
M2 = 128
MW = 48
NB = 9
W_ROWS = 40
LEVEL_PAIRS = ((0, 0), (0, 1), (1, 0), (1, 1), (1, 2), (2, 1), (2, 2), (2, 3), (3, 2), (3, 3))


def column_bases():
    base = np.zeros((6, 6), np.int32)
    for a in range(6):
        for b in range(6):
            if a == 0:
                base[a, b] = 96 + b * 4
            elif a == 5:
                base[a, b] = 120 + b * 4
            elif b == 0:
                base[a, b] = 64 + (a - 1) * 4
            elif b == 5:
                base[a, b] = 80 + (a - 1) * 4
            else:
                base[a, b] = ((a - 1) * 4 + (b - 1)) * 4
    return base


def item_table(columns):
    base = column_bases()
    rows = []
    for c, d in LEVEL_PAIRS:
        for a, b in columns:
            row = [((a - 1) * 4 + (b - 1)) * 4 + c]
            for da in (-1, 0, 1):
                for db in (-1, 0, 1):
                    row.append(base[a + da, b + db] + d)
            rows.append(row)
    return np.asarray(rows, np.int32).reshape(-1)


def spread_matrix():
    out = np.zeros((32, 256), np.float32)
    for g in range(9):
        for r in range(8):
            out[(g // 3) * 8 + r, g * 8 + r] = 1.0
    for r in range(8):
        out[24 + r, 72 + r] = 1.0
    out[[6, 14, 22], 128:] = 1.0
    return out


def split3(x):
    h = x.astype(BF16).astype(F32)
    r = x - h
    m = r.astype(BF16).astype(F32)
    return h, m, r - m


def pair_rows(state, corner, spread, k, with_targets, rows_ref, a_ref, b_ref, rho_ref):
    blk = pl.ds(pl.multiple_of(k * 8, 8), 8)
    x = [state[d, blk, :] - corner[d] for d in range(3)]
    v = [state[3 + d, blk, :] for d in range(3)]
    rho = state[6, blk, :]
    n2 = x[0] * x[0] + x[1] * x[1] + x[2] * x[2]
    xv = x[0] * v[0] + x[1] * v[1] + x[2] * v[2]
    one = jnp.ones_like(n2)
    zero = jnp.zeros_like(n2)
    xs = [split3(t) for t in x]
    vs = [split3(t) for t in v]
    rs = split3(rho)
    n2s = split3(n2)
    xvs = split3(xv)

    def put(group, parts):
        for r, p in enumerate(parts):
            rows_ref[pl.ds((group * 8 + r) * 8, 8), :] = p

    def get(group, b):
        return rows_ref[pl.ds(group * 64 + b, 8, stride=8), :]

    for s in range(3):
        put(s, [xs[d][s] for d in range(3)] + [vs[d][s] for d in range(3)] + [rs[s], one])
    put(3, list(n2s) + list(xvs) + [one, one])
    if with_targets:
        for s in range(3):
            put(4 + s, [-0.5 * xs[d][s] for d in range(3)] + [zero] * 5)
            put(7 + s, [-vs[d][s] for d in range(3)] + [-xs[d][s] for d in range(3)] + [zero] * 2)
        quarter = one * 0.25
        put(10, [-0.5 * xs[d][0] for d in range(3)] + [zero] * 4 + [0.25 * n2s[2]])
        put(11, [-vs[d][0] for d in range(3)] + [-xs[d][0] for d in range(3)] + [zero, xvs[2]])
        put(12, [quarter] * 3 + [zero] * 3 + [0.25 * n2s[0], 0.25 * n2s[1]])
        put(13, [zero] * 3 + [one] * 3 + [xvs[0], xvs[1]])
    cols = [jnp.concatenate([get(s, b) for s in range(4)], 0).T.astype(BF16) for b in range(8)]
    both = jnp.dot(jnp.concatenate(cols, 0), spread, preferred_element_type=F32)
    for b in range(8):
        rows = slice(b * 128, b * 128 + 128)
        a_ref[k * 8 + b] = both[rows, :KA].astype(BF16)
        if rho_ref is not None:
            rho_ref[k * 8 + b] = both[rows, 128:]
        if with_targets:
            r2_rows = [get(10, b), get(5, b), get(6, b)] + [get(4 + s, b) for s in range(3)] * 2
            b_ref[k * 8 + b, :, :128] = jnp.concatenate(r2_rows + [get(12, b)], 0).astype(BF16)
            if rho_ref is not None:
                vx_rows = [get(11, b), get(8, b), get(9, b)] + [get(7 + s, b) for s in range(3)] * 2
                b_ref[k * 8 + b, :, 128:] = jnp.concatenate(vx_rows + [get(13, b)], 0).astype(BF16)


def store_features(rows_ref, out_ref, k, features, rows, first):
    at = first
    for f in features:
        for piece in split3(f):
            rows_ref[pl.ds(at * 8, 8), :] = piece
            at += 1
    return at


def gather_features(rows_ref, out_ref, k, rows):
    for b in range(8):
        out_ref[k * 8 + b] = rows_ref[pl.ds(b, rows, stride=8), :].astype(BF16)


def hi_lo(x):
    hi = x.astype(BF16)
    return hi, (x - hi.astype(F32)).astype(BF16)


def falloff_cubed(s2):
    q = jnp.maximum(1.0 - s2 * lax.rsqrt(s2), 0.0)
    return q * q * q


CHUNKS = ((0, 2), (2, 4), (4, 6), (6, 8), (8, 9))


def for_items(n, one, rest):
    one(0, 0)
    one(1, 1)

    def step(s, carry):
        t = 4 * s
        for e in range(4):
            one(jnp.minimum(t + e + 2, n - 1), (e + 2) % 4)
            rest(t + e, e)
        return carry

    lax.fori_loop(0, n // 4, step, 0)


def moment_kernel(n_ref, tab, corner_ref, spread_ref, state, corr, a_ref, b_ref, f_ref, rows_ref, r_ref, acc):
    corner = [corner_ref[d] for d in range(3)]
    n = n_ref[0]
    spread = spread_ref[...]

    def prepare(k, with_targets):
        pair_rows(state, corner, spread, k, with_targets, rows_ref, a_ref, b_ref, None)
        blk = pl.ds(pl.multiple_of(k * 8, 8), 8)
        x = [state[d, blk, :] - corner[d] for d in range(3)]
        vol = state[7, blk, :] / state[6, blk, :]
        vx = [vol * t for t in x]
        features = [vol] + vx + [vx[p] * x[q] for p, q in SYM_PAIRS]
        at = store_features(rows_ref, f_ref, k, features, M1, 0)
        for r in range(at, M1):
            rows_ref[pl.ds(r * 8, 8), :] = jnp.zeros((8, 128), F32)
        gather_features(rows_ref, f_ref, k, M1)

    def first(k, carry):
        prepare(k, True)
        return carry

    def others(k, carry):
        prepare(k, False)
        return carry

    lax.fori_loop(0, LOCAL // 8, first, 0)
    lax.fori_loop(LOCAL // 8, TOTAL // 8, others, 0)
    acc[...] = jnp.zeros_like(acc)

    def one(t, p):
        for c in CHUNKS:
            lhs = jnp.concatenate([a_ref[tab[t * 10 + 1 + e]] for e in range(*c)], 0)
            rows = pl.ds(c[0] * 128, (c[1] - c[0]) * 128)
            r_ref[p, rows, :] = jnp.dot(lhs, b_ref[tab[t * 10]], preferred_element_type=F32)

    def rest(t, p):
        i = tab[t * 10]
        partner = [tab[t * 10 + 1 + e] for e in range(NB)]
        weights = []
        for c in CHUNKS:
            s2 = jnp.maximum(r_ref[p, pl.ds(c[0] * 128, (c[1] - c[0]) * 128), :], TINY)
            weights.append(jnp.concatenate(hi_lo(falloff_cubed(s2)), 1))
        lhs = jnp.concatenate([f_ref[j] for j in partner], 1)
        part = jnp.dot(lhs, jnp.concatenate(weights, 0), preferred_element_type=F32)
        acc[pl.ds(pl.multiple_of(i * M1, M1), M1), :] += part[:, :128] + part[:, 128:]

    for_items(n, one, rest)

    def finish(k, carry):
        blk = pl.ds(pl.multiple_of(k * 8, 8), 8)
        x = [state[d, blk, :] - corner[d] for d in range(3)]

        def total(f):
            at = [acc[pl.ds(k * (8 * M1) + 3 * f + s, 8, stride=M1), :] for s in range(3)]
            return at[0] + (at[1] + at[2])

        t0 = total(0)
        t1 = [total(1 + d) for d in range(3)]
        mom = []
        for e, (p, q) in enumerate(SYM_PAIRS):
            value = (x[p] * t0 - t1[p]) * x[q] + (total(4 + e) - x[p] * t1[q])
            mom.append(KERNEL_GRAD * value)
        a, d, f = (mom[e] + REGULAR for e in range(3))
        b, c, e = mom[3:]
        cof_xx = d * f - e * e
        cof_xy = c * e - b * f
        cof_xz = b * e - c * d
        cof_yy = a * f - c * c
        cof_yz = b * c - a * e
        cof_zz = a * d - b * b
        scale = 1.0 / (a * cof_xx + b * cof_xy + c * cof_xz)
        for r, cof in enumerate((cof_xx, cof_yy, cof_zz, cof_xy, cof_xz, cof_yz)):
            corr[r, blk, :] = cof * scale
        return carry

    lax.fori_loop(0, LOCAL // 8, finish, 0)


def rate_kernel(n_ref, tab, corner_ref, spread_ref, state, corr, rate, a_ref, b_ref, rho_ref, f_ref, rows_ref, r_ref, acc,
                accw):
    corner = [corner_ref[d] for d in range(3)]
    n = n_ref[0]
    spread = spread_ref[...]

    def pressure(rho):
        r2 = rho * rho
        return STIFFNESS * (r2 * r2 * r2 * rho - 1.0) / r2

    def times(sym, vec):
        return [sym[SYM_INDEX[p][0]] * vec[0] + sym[SYM_INDEX[p][1]] * vec[1] + sym[SYM_INDEX[p][2]] * vec[2]
                for p in range(3)]

    def prepare(k, with_targets):
        pair_rows(state, corner, spread, k, with_targets, rows_ref, a_ref, b_ref, rho_ref)
        blk = pl.ds(pl.multiple_of(k * 8, 8), 8)
        x = [state[d, blk, :] - corner[d] for d in range(3)]
        v = [state[3 + d, blk, :] for d in range(3)]
        rho = state[6, blk, :]
        m = state[7, blk, :]
        sym = [corr[r, blk, :] for r in range(6)]
        m_sym = [m * t for t in sym]
        m_sym_x = times(m_sym, x)
        m_sym_v = times(m_sym, v)
        prs = pressure(rho)
        mp = m * prs
        mv = [m * t for t in v]
        shared = [m] + [m * t for t in x] + m_sym + m_sym_x
        own = (mv + [mv[p] * x[q] for p in range(3) for q in range(3)] + m_sym_v
               + [v[0] * m_sym_x[0] + v[1] * m_sym_x[1] + v[2] * m_sym_x[2]]
               + [mp] + [mp * t for t in x] + [prs * t for t in m_sym] + [prs * t for t in m_sym_x])
        at = store_features(rows_ref, f_ref, k, shared, M2, 0)
        for r in range(at, W_ROWS):
            rows_ref[pl.ds(r * 8, 8), :] = jnp.zeros((8, 128), F32)
        at = store_features(rows_ref, f_ref, k, own, M2, W_ROWS)
        for r in range(at, M2):
            rows_ref[pl.ds(r * 8, 8), :] = jnp.zeros((8, 128), F32)
        gather_features(rows_ref, f_ref, k, M2)

    def first(k, carry):
        prepare(k, True)
        return carry

    def others(k, carry):
        prepare(k, False)
        return carry

    lax.fori_loop(0, LOCAL // 8, first, 0)
    lax.fori_loop(LOCAL // 8, TOTAL // 8, others, 0)
    acc[...] = jnp.zeros_like(acc)
    accw[...] = jnp.zeros_like(accw)

    def one(t, p):
        for c in CHUNKS:
            lhs = jnp.concatenate([a_ref[tab[t * 10 + 1 + e]] for e in range(*c)], 0)
            rows = pl.ds(c[0] * 128, (c[1] - c[0]) * 128)
            r_ref[p, rows, :] = jnp.dot(lhs, b_ref[tab[t * 10]], preferred_element_type=F32)

    def rest(t, p):
        i = tab[t * 10]
        partner = [tab[t * 10 + 1 + e] for e in range(NB)]
        rho_i = state[6, pl.ds(i, 1), :]
        weights = []
        viscous = []
        for c in CHUNKS:
            both = r_ref[p, pl.ds(c[0] * 128, (c[1] - c[0]) * 128), :]
            s2 = jnp.maximum(both[:, :128], TINY)
            fall = falloff_cubed(s2)
            weights.append(jnp.concatenate(hi_lo(fall), 1))
            rho_j = jnp.concatenate([rho_ref[partner[e]] for e in range(*c)], 0)
            bottom = (s2 + 0.25 * SOFTEN) * (rho_j + rho_i)
            w = fall * jnp.minimum(both[:, 128:], 0.0) * pltpu.reciprocal(bottom)
            viscous.append(jnp.concatenate(hi_lo(w), 1))
        lhs = jnp.concatenate([f_ref[j] for j in partner], 1)
        part = jnp.dot(lhs, jnp.concatenate(weights, 0), preferred_element_type=F32)
        acc[pl.ds(pl.multiple_of(i * M2, M2), M2), :] += part[:, :128] + part[:, 128:]
        part = jnp.dot(lhs[:MW], jnp.concatenate(viscous, 0), preferred_element_type=F32)
        accw[pl.ds(pl.multiple_of(i * MW, MW), MW), :] += part[:, :128] + part[:, 128:]

    for_items(n, one, rest)

    def finish(k, carry):
        blk = pl.ds(pl.multiple_of(k * 8, 8), 8)
        x = [state[d, blk, :] - corner[d] for d in range(3)]
        v = [state[3 + d, blk, :] for d in range(3)]
        prs = pressure(state[6, blk, :])
        sym = [corr[r, blk, :] for r in range(6)]

        def total(ref, height, first_row, f):
            at = [ref[pl.ds(k * (8 * height) + first_row + 3 * f + s, 8, stride=height), :] for s in range(3)]
            return at[0] + (at[1] + at[2])

        shared = [total(acc, M2, 0, f) for f in range(13)]
        own = [total(acc, M2, W_ROWS, f) for f in range(29)]
        visc = [total(accw, MW, 0, f) for f in range(13)]
        m0, mx, mk, mkx = shared[0], shared[1:4], shared[4:10], shared[10:13]
        mv, mvx, mkv, mvkx = own[0:3], own[3:12], own[12:15], own[15]
        p0, px, pk, pkx = own[16], own[17:20], own[20:26], own[26:29]
        w0, wx, wk, wkx = visc[0], visc[1:4], visc[4:10], visc[10:13]
        vx = [[v[p] * (x[q] * m0 - mx[q]) - (mv[p] * x[q] - mvx[3 * p + q]) for q in range(3)] for p in range(3)]
        inner = jnp.zeros_like(m0)
        for p in range(3):
            for q in range(3):
                inner = inner + sym[SYM_INDEX[p][q]] * vx[p][q]
        mk_x = times(mk, x)
        for p in range(3):
            inner = inner + v[p] * (mk_x[p] - mkx[p]) - x[p] * mkv[p]
        inner = inner + mvkx
        rate[0, blk, :] = (-0.5 * KERNEL_GRAD) * inner
        near = [prs * (x[p] * m0 - mx[p]) + (x[p] * p0 - px[p]) - 0.25 * (x[p] * w0 - wx[p]) for p in range(3)]
        mine = times(sym, near)
        pk_x = times(pk, x)
        wk_x = times(wk, x)
        for p in range(3):
            far = prs * (mk_x[p] - mkx[p]) + (pk_x[p] - pkx[p]) - 0.25 * (wk_x[p] - wkx[p])
            rate[1 + p, blk, :] = (0.5 * KERNEL_GRAD) * (mine[p] + far)
        return carry

    lax.fori_loop(0, LOCAL // 8, finish, 0)


VMEM = pl.BlockSpec(memory_space=pltpu.VMEM)
SMEM = pl.BlockSpec(memory_space=pltpu.SMEM)
ALL_COLUMNS = tuple((a, b) for a in range(1, 5) for b in range(1, 5))


def run_moments(n, table, corner, state):
    return pl.pallas_call(
        moment_kernel,
        out_shape=jax.ShapeDtypeStruct((6, LOCAL, 128), F32),
        in_specs=[SMEM, SMEM, SMEM, VMEM, VMEM],
        out_specs=VMEM,
        scratch_shapes=[
            pltpu.VMEM((TOTAL, 128, KA), BF16),
            pltpu.VMEM((LOCAL, KA, 128), BF16),
            pltpu.VMEM((TOTAL, M1, 128), BF16),
            pltpu.VMEM((14 * 64, 128), F32),
            pltpu.VMEM((4, NB * 128, 128), F32),
            pltpu.VMEM((LOCAL * M1, 128), F32),
        ],
        compiler_params=pltpu.CompilerParams(vmem_limit_bytes=56 * 2**20),
        name="moments",
    )(n, table, corner, jnp.asarray(spread_matrix(), BF16), state)


def run_rates(n, table, corner, state, corr):
    return pl.pallas_call(
        rate_kernel,
        out_shape=jax.ShapeDtypeStruct((4, LOCAL, 128), F32),
        in_specs=[SMEM, SMEM, SMEM, VMEM, VMEM, VMEM],
        out_specs=VMEM,
        scratch_shapes=[
            pltpu.VMEM((TOTAL, 128, KA), BF16),
            pltpu.VMEM((LOCAL, KA, 256), BF16),
            pltpu.VMEM((TOTAL, 128, 128), F32),
            pltpu.VMEM((TOTAL, M2, 128), BF16),
            pltpu.VMEM((M2 * 8, 128), F32),
            pltpu.VMEM((4, NB * 128, 256), F32),
            pltpu.VMEM((LOCAL * M2, 128), F32),
            pltpu.VMEM((LOCAL * MW, 128), F32),
        ],
        compiler_params=pltpu.CompilerParams(vmem_limit_bytes=60 * 2**20),
        name="rates",
    )(n, table, corner, jnp.asarray(spread_matrix(), BF16), state, corr)


def shifted(value, axis, steps):
    count = lax.axis_size(axis)
    first, last = (max(0, -steps), min(count, count - steps))
    return lax.ppermute(value, axis, [(source, source + steps) for source in range(first, last)])


def with_halo(blocks):
    ch = blocks.shape[0]
    low_y = shifted(blocks[:, :, -1:], "gy", 1)
    high_y = shifted(blocks[:, :, :1], "gy", -1)

    def row(a):
        return jnp.concatenate([low_y[:, a:a + 1], blocks[:, a:a + 1], high_y[:, a:a + 1]], 2)

    low_x = shifted(row(3), "gx", 1)
    high_x = shifted(row(0), "gx", -1)
    return jnp.concatenate([t.reshape(ch, -1, 128) for t in (blocks, low_y, high_y, low_x, high_x)], 1)


def occupied_levels(mass):
    any_live = jnp.max(mass.reshape(TOTAL // 4, 4, 128), axis=(0, 2)) > 0.0
    return jnp.max(jnp.where(any_live, jnp.arange(1, 5, dtype=jnp.int32), 1))


def body(positions, velocity, density, masses, counts):
    shape = density.shape
    live = lax.broadcasted_iota(jnp.int32, shape, 3) < counts[..., None]
    blocks = jnp.concatenate(
        [
            jnp.where(live, positions, 0.0),
            jnp.where(live, velocity, 0.0),
            jnp.where(live, density, 1.0)[None],
            jnp.where(live, masses, 0.0)[None],
        ],
        0,
    )
    state = with_halo(blocks)
    state = state.at[6].set(jnp.where(state[6] > 0.0, state[6], 1.0))
    centre_x = (lax.axis_index("gx") * 8 + 4).astype(F32)
    centre_y = (lax.axis_index("gy") * 8 + 4).astype(F32)
    corner = jnp.stack([centre_x, centre_y, jnp.float32(4.0)])
    table = jnp.asarray(item_table(ALL_COLUMNS))
    n = ((3 * occupied_levels(state[7]) - 2) * 16).reshape(1)
    corr = run_moments(n, table, corner, state)
    corr_all = with_halo(corr.reshape((6,) + shape))
    rates = run_rates(n, table, corner, state, corr_all).reshape((4,) + shape)
    density_rate = jnp.where(live, rates[0], 0.0)
    pull = jnp.asarray([0.0, 0.0, -GRAVITY], F32).reshape(3, 1, 1, 1, 1)
    acceleration = jnp.where(live, rates[1:4] + pull, 0.0)
    return (density_rate, acceleration)


def solution(mesh):
    return jax.shard_map(
        body,
        mesh=mesh,
        in_specs=(
            P(None, "gx", "gy", None, None),
            P(None, "gx", "gy", None, None),
            P("gx", "gy", None, None),
            P("gx", "gy", None, None),
            P("gx", "gy", None),
        ),
        out_specs=(P("gx", "gy", None, None), P(None, "gx", "gy", None, None)),
        check_vma=False,
    )
```

```python
import functools
import math

import jax
import jax.numpy as jnp
import numpy as np
from jax import lax
from jax.experimental import pallas as pl
from jax.experimental.pallas import tpu as pltpu
from jax.sharding import PartitionSpec as P

KERNEL_GRAD = 105.0 / (16.0 * math.pi)
REGULAR = 0.2
STIFFNESS = 100.0 / 7.0
GRAVITY = 1.0
SOFTEN = 0.01
TINY = 1e-12
SYM_PAIRS = ((0, 0), (1, 1), (2, 2), (0, 1), (0, 2), (1, 2))
SYM_INDEX = ((0, 3, 4), (3, 1, 5), (4, 5, 2))
F32 = jnp.float32
BF16 = jnp.bfloat16
LOCAL = 64
TOTAL = 144
KA = 80
M1 = 32
M2 = 128
MW = 48
NB = 9
W_ROWS = 40
LEVEL_PAIRS = ((0, 0), (0, 1), (1, 0), (1, 1), (1, 2), (2, 1), (2, 2), (2, 3), (3, 2), (3, 3))


def column_bases():
    base = np.zeros((6, 6), np.int32)
    for a in range(6):
        for b in range(6):
            if a == 0:
                base[a, b] = 96 + b * 4
            elif a == 5:
                base[a, b] = 120 + b * 4
            elif b == 0:
                base[a, b] = 64 + (a - 1) * 4
            elif b == 5:
                base[a, b] = 80 + (a - 1) * 4
            else:
                base[a, b] = ((a - 1) * 4 + (b - 1)) * 4
    return base


def item_table(columns):
    base = column_bases()
    rows = []
    for c, d in LEVEL_PAIRS:
        for a, b in columns:
            row = [((a - 1) * 4 + (b - 1)) * 4 + c]
            for da in (-1, 0, 1):
                for db in (-1, 0, 1):
                    row.append(base[a + da, b + db] + d)
            rows.append(row)
    return np.asarray(rows, np.int32).reshape(-1)


def spread_matrix():
    out = np.zeros((32, 256), np.float32)
    for g in range(9):
        for r in range(8):
            out[(g // 3) * 8 + r, g * 8 + r] = 1.0
    for r in range(8):
        out[24 + r, 72 + r] = 1.0
    out[[6, 14, 22], 128:] = 1.0
    return out


def split3(x):
    h = x.astype(BF16).astype(F32)
    r = x - h
    m = r.astype(BF16).astype(F32)
    return h, m, r - m


def fixed_rows(rows_ref):
    rows_ref[...] = jnp.zeros_like(rows_ref)
    rows_ref[pl.ds(7 * 8, 8), :] = jnp.ones((8, 128), F32)


def pair_rows(state, corner, spread, k, with_targets, rows_ref, a_ref, b_ref, rho_ref):
    blk = pl.ds(pl.multiple_of(k * 8, 8), 8)
    x = [state[d, blk, :] - corner[d] for d in range(3)]
    v = [state[3 + d, blk, :] for d in range(3)]
    n2s = split3(x[0] * x[0] + x[1] * x[1] + x[2] * x[2])
    xvs = split3(x[0] * v[0] + x[1] * v[1] + x[2] * v[2])
    xs = [split3(t) for t in x]
    vs = [split3(t) for t in v]
    rs = split3(state[6, blk, :])

    def put(group, row, parts):
        for r, p in enumerate(parts):
            rows_ref[pl.ds((group * 8 + row + r) * 8, 8), :] = p

    def get(group, b):
        return rows_ref[pl.ds(group * 64 + b, 8, stride=8), :]

    for s in range(3):
        put(s, 0, [xs[d][s] for d in range(3)] + [vs[d][s] for d in range(3)] + [rs[s]])
    put(3, 0, n2s + xvs)
    if with_targets:
        for s in range(3):
            put(4 + s, 0, [-0.5 * xs[d][s] for d in range(3)])
            put(4 + s, 7, [0.25 * n2s[s]])
            if rho_ref is not None:
                put(7 + s, 0, [-vs[d][s] for d in range(3)] + [-xs[d][s] for d in range(3)])
                put(7 + s, 7, [xvs[s]])
        row = lax.broadcasted_iota(jnp.int32, (8, 128), 0)
        quarters = jnp.where(row < 3, 0.25, 0.0)
        ones = jnp.where((row >= 3) & (row < 6), 1.0, 0.0)
    cols = [jnp.concatenate([get(s, b) for s in range(4)], 0).T.astype(BF16) for b in range(8)]
    both = jnp.dot(jnp.concatenate(cols, 0), spread, preferred_element_type=F32)
    for b in range(8):
        rows = slice(b * 128, b * 128 + 128)
        a_ref[k * 8 + b] = both[rows, :KA].astype(BF16)
        if rho_ref is not None:
            rho_ref[k * 8 + b] = both[rows, 128:]
        if with_targets:
            r2_rows = [get(4 + s, b) for s in range(3)] * 3
            b_ref[k * 8 + b, :, :128] = jnp.concatenate(r2_rows + [quarters], 0).astype(BF16)
            if rho_ref is not None:
                vx_rows = [get(7 + s, b) for s in range(3)] * 3
                b_ref[k * 8 + b, :, 128:] = jnp.concatenate(vx_rows + [ones], 0).astype(BF16)


def gather_blocks(parts, state):
    at = 0
    for part in parts:
        for k in range(part.shape[1] // 8):
            yield part, pl.ds(k * 8, 8), pl.ds(at, 8)
            at += 8


def load_state(parts, state):
    peak = jnp.zeros((8, 128), F32)
    for part, src, dst in gather_blocks(parts, state):
        mass = part[7, src, :]
        live = mass > 0.0
        for d in range(6):
            state[d, dst, :] = jnp.where(live, part[d, src, :], 0.0)
        state[6, dst, :] = jnp.where(live, part[6, src, :], 1.0)
        state[7, dst, :] = mass
        peak = jnp.maximum(peak, mass)
    level = (lax.broadcasted_iota(jnp.int32, (8, 128), 0) % 4 + 1).astype(F32)
    return jnp.max(jnp.where(peak > 0.0, level, 1.0)).astype(jnp.int32)


def centre():
    return [(lax.axis_index("gx") * 8 + 4).astype(F32), (lax.axis_index("gy") * 8 + 4).astype(F32), 4.0]


def unfold(src, height, k, rows_ref):
    for b in range(8):
        for g in range(height // 8):
            rows = pl.ds(pl.multiple_of((k * 8 + b) * height, height) + g * 8, 8)
            rows_ref[pl.ds(g * 64 + b, 8, stride=8), :] = src[rows, :]


def store_features(rows_ref, features, at):
    for f in features:
        for piece in split3(f):
            rows_ref[pl.ds(at * 8, 8), :] = piece
            at += 1


def gather_features(rows_ref, out_ref, k, rows):
    for b in range(8):
        out_ref[k * 8 + b] = rows_ref[pl.ds(b, rows, stride=8), :].astype(BF16)


def hi_lo(x):
    hi = x.astype(BF16)
    return hi, (x - hi.astype(F32)).astype(BF16)


def falloff_cubed(s2):
    q = jnp.maximum(1.0 - s2 * lax.rsqrt(s2), 0.0)
    return q * q * q


CHUNKS = ((0, 2), (2, 4), (4, 6), (6, 8), (8, 9))


def for_items(n, one, rest):
    one(0, 0)
    one(1, 1)

    def step(s, carry):
        t = 4 * s
        for e in range(4):
            one(jnp.minimum(t + e + 2, n - 1), (e + 2) % 4)
            rest(t + e, e)
        return carry

    lax.fori_loop(0, n // 4, step, 0)


def moment_kernel(tab, spread_ref, local, low_y, high_y, low_x, high_x, corr, state, a_ref, b_ref, f_ref, rows_ref,
                  feat_ref, r_ref, acc):
    corner = centre()
    levels = load_state((local, low_y, high_y, low_x, high_x), state)
    n = (3 * levels - 2) * 16
    spread = spread_ref[...]
    fixed_rows(rows_ref)
    feat_ref[...] = jnp.zeros_like(feat_ref)

    def prepare(k, with_targets):
        pair_rows(state, corner, spread, k, with_targets, rows_ref, a_ref, b_ref, None)
        blk = pl.ds(pl.multiple_of(k * 8, 8), 8)
        x = [state[d, blk, :] - corner[d] for d in range(3)]
        vol = state[7, blk, :] / state[6, blk, :]
        vx = [vol * t for t in x]
        features = [vol] + vx + [vx[p] * x[q] for p, q in SYM_PAIRS]
        store_features(feat_ref, features, 0)
        gather_features(feat_ref, f_ref, k, M1)

    def first(k, carry):
        prepare(k, True)
        return carry

    def others(k, carry):
        prepare(k, False)
        return carry

    lax.fori_loop(0, LOCAL // 8, first, 0)
    lax.fori_loop(LOCAL // 8, TOTAL // 8, others, 0)
    acc[...] = jnp.zeros_like(acc)

    def one(t, p):
        for c in CHUNKS:
            lhs = jnp.concatenate([a_ref[tab[t * 10 + 1 + e]] for e in range(*c)], 0)
            rows = pl.ds(c[0] * 128, (c[1] - c[0]) * 128)
            r_ref[p, rows, :] = jnp.dot(lhs, b_ref[tab[t * 10]], preferred_element_type=F32)

    def rest(t, p):
        i = tab[t * 10]
        partner = [tab[t * 10 + 1 + e] for e in range(NB)]
        weights = []
        for c in CHUNKS:
            s2 = jnp.maximum(r_ref[p, pl.ds(c[0] * 128, (c[1] - c[0]) * 128), :], TINY)
            weights.append(jnp.concatenate(hi_lo(falloff_cubed(s2)), 1))
        lhs = jnp.concatenate([f_ref[j] for j in partner], 1)
        part = jnp.dot(lhs, jnp.concatenate(weights, 0), preferred_element_type=F32)
        acc[pl.ds(pl.multiple_of(i * M1, M1), M1), :] += part[:, :128] + part[:, 128:]

    for_items(n, one, rest)

    def finish(k, carry):
        unfold(acc, M1, k, feat_ref)
        blk = pl.ds(pl.multiple_of(k * 8, 8), 8)
        x = [state[d, blk, :] - corner[d] for d in range(3)]

        def total(f):
            at = [feat_ref[pl.ds((3 * f + s) * 8, 8), :] for s in range(3)]
            return at[0] + (at[1] + at[2])

        t0 = total(0)
        t1 = [total(1 + d) for d in range(3)]
        mom = []
        for e, (p, q) in enumerate(SYM_PAIRS):
            value = (x[p] * t0 - t1[p]) * x[q] + (total(4 + e) - x[p] * t1[q])
            mom.append(KERNEL_GRAD * value)
        a, d, f = (mom[e] + REGULAR for e in range(3))
        b, c, e = mom[3:]
        cof_xx = d * f - e * e
        cof_xy = c * e - b * f
        cof_xz = b * e - c * d
        cof_yy = a * f - c * c
        cof_yz = b * c - a * e
        cof_zz = a * d - b * b
        scale = 1.0 / (a * cof_xx + b * cof_xy + c * cof_xz)
        for r, cof in enumerate((cof_xx, cof_yy, cof_zz, cof_xy, cof_xz, cof_yz)):
            corr[r, blk, :] = cof * scale
        return carry

    lax.fori_loop(0, LOCAL // 8, finish, 0)


def rate_kernel(tab, spread_ref, local, low_y, high_y, low_x, high_x, corr0, corr1, corr2, corr3, corr4, rate, accel,
                state, corr, a_ref, b_ref, rho_ref, f_ref, rows_ref, feat_ref, featw_ref, r_ref, acc, accw):
    corner = centre()
    levels = load_state((local, low_y, high_y, low_x, high_x), state)
    n = (3 * levels - 2) * 16
    spread = spread_ref[...]
    fixed_rows(rows_ref)
    feat_ref[...] = jnp.zeros_like(feat_ref)
    for part, src, dst in gather_blocks((corr0, corr1, corr2, corr3, corr4), corr):
        for d in range(6):
            corr[d, dst, :] = part[d, src, :]

    def pressure(rho):
        r2 = rho * rho
        return STIFFNESS * (r2 * r2 * r2 * rho - 1.0) / r2

    def times(sym, vec):
        return [sym[SYM_INDEX[p][0]] * vec[0] + sym[SYM_INDEX[p][1]] * vec[1] + sym[SYM_INDEX[p][2]] * vec[2]
                for p in range(3)]

    def prepare(k, with_targets):
        pair_rows(state, corner, spread, k, with_targets, rows_ref, a_ref, b_ref, rho_ref)
        blk = pl.ds(pl.multiple_of(k * 8, 8), 8)
        x = [state[d, blk, :] - corner[d] for d in range(3)]
        v = [state[3 + d, blk, :] for d in range(3)]
        rho = state[6, blk, :]
        m = state[7, blk, :]
        sym = [corr[r, blk, :] for r in range(6)]
        m_sym = [m * t for t in sym]
        m_sym_x = times(m_sym, x)
        m_sym_v = times(m_sym, v)
        prs = pressure(rho)
        mp = m * prs
        mv = [m * t for t in v]
        shared = [m] + [m * t for t in x] + m_sym + m_sym_x
        own = (mv + [mv[p] * x[q] for p in range(3) for q in range(3)] + m_sym_v
               + [v[0] * m_sym_x[0] + v[1] * m_sym_x[1] + v[2] * m_sym_x[2]]
               + [mp] + [mp * t for t in x] + [prs * t for t in m_sym] + [prs * t for t in m_sym_x])
        store_features(feat_ref, shared, 0)
        store_features(feat_ref, own, W_ROWS)
        gather_features(feat_ref, f_ref, k, M2)

    def first(k, carry):
        prepare(k, True)
        return carry

    def others(k, carry):
        prepare(k, False)
        return carry

    lax.fori_loop(0, LOCAL // 8, first, 0)
    lax.fori_loop(LOCAL // 8, TOTAL // 8, others, 0)
    acc[...] = jnp.zeros_like(acc)
    accw[...] = jnp.zeros_like(accw)

    def one(t, p):
        for c in CHUNKS:
            lhs = jnp.concatenate([a_ref[tab[t * 10 + 1 + e]] for e in range(*c)], 0)
            rows = pl.ds(c[0] * 128, (c[1] - c[0]) * 128)
            r_ref[p, rows, :] = jnp.dot(lhs, b_ref[tab[t * 10]], preferred_element_type=F32)

    def rest(t, p):
        i = tab[t * 10]
        partner = [tab[t * 10 + 1 + e] for e in range(NB)]
        rho_i = state[6, pl.ds(i, 1), :]
        weights = []
        viscous = []
        for c in CHUNKS:
            both = r_ref[p, pl.ds(c[0] * 128, (c[1] - c[0]) * 128), :]
            s2 = jnp.maximum(both[:, :128], TINY)
            fall = falloff_cubed(s2)
            weights.append(jnp.concatenate(hi_lo(fall), 1))
            rho_j = jnp.concatenate([rho_ref[partner[e]] for e in range(*c)], 0)
            bottom = (s2 + 0.25 * SOFTEN) * (rho_j + rho_i)
            w = fall * jnp.minimum(both[:, 128:], 0.0) * pltpu.reciprocal(bottom)
            viscous.append(jnp.concatenate(hi_lo(w), 1))
        lhs = jnp.concatenate([f_ref[j] for j in partner], 1)
        part = jnp.dot(lhs, jnp.concatenate(weights, 0), preferred_element_type=F32)
        acc[pl.ds(pl.multiple_of(i * M2, M2), M2), :] += part[:, :128] + part[:, 128:]
        part = jnp.dot(lhs[:MW], jnp.concatenate(viscous, 0), preferred_element_type=F32)
        accw[pl.ds(pl.multiple_of(i * MW, MW), MW), :] += part[:, :128] + part[:, 128:]

    for_items(n, one, rest)

    def finish(k, carry):
        unfold(acc, M2, k, feat_ref)
        unfold(accw, MW, k, featw_ref)
        blk = pl.ds(pl.multiple_of(k * 8, 8), 8)
        x = [state[d, blk, :] - corner[d] for d in range(3)]
        v = [state[3 + d, blk, :] for d in range(3)]
        prs = pressure(state[6, blk, :])
        sym = [corr[r, blk, :] for r in range(6)]

        def total(ref, first_row, f):
            at = [ref[pl.ds((first_row + 3 * f + s) * 8, 8), :] for s in range(3)]
            return at[0] + (at[1] + at[2])

        shared = [total(feat_ref, 0, f) for f in range(13)]
        own = [total(feat_ref, W_ROWS, f) for f in range(29)]
        visc = [total(featw_ref, 0, f) for f in range(13)]
        m0, mx, mk, mkx = shared[0], shared[1:4], shared[4:10], shared[10:13]
        mv, mvx, mkv, mvkx = own[0:3], own[3:12], own[12:15], own[15]
        p0, px, pk, pkx = own[16], own[17:20], own[20:26], own[26:29]
        w0, wx, wk, wkx = visc[0], visc[1:4], visc[4:10], visc[10:13]
        vx = [[v[p] * (x[q] * m0 - mx[q]) - (mv[p] * x[q] - mvx[3 * p + q]) for q in range(3)] for p in range(3)]
        inner = jnp.zeros_like(m0)
        for p in range(3):
            for q in range(3):
                inner = inner + sym[SYM_INDEX[p][q]] * vx[p][q]
        mk_x = times(mk, x)
        for p in range(3):
            inner = inner + v[p] * (mk_x[p] - mkx[p]) - x[p] * mkv[p]
        inner = inner + mvkx
        live = state[7, blk, :] > 0.0
        rate[blk, :] = jnp.where(live, (-0.5 * KERNEL_GRAD) * inner, 0.0)
        near = [prs * (x[p] * m0 - mx[p]) + (x[p] * p0 - px[p]) - 0.25 * (x[p] * w0 - wx[p]) for p in range(3)]
        mine = times(sym, near)
        pk_x = times(pk, x)
        wk_x = times(wk, x)
        for p in range(3):
            far = prs * (mk_x[p] - mkx[p]) + (pk_x[p] - pkx[p]) - 0.25 * (wk_x[p] - wkx[p])
            pull = -GRAVITY if p == 2 else 0.0
            accel[p, blk, :] = jnp.where(live, (0.5 * KERNEL_GRAD) * (mine[p] + far) + pull, 0.0)
        return carry

    lax.fori_loop(0, LOCAL // 8, finish, 0)


VMEM = pl.BlockSpec(memory_space=pltpu.VMEM)
SMEM = pl.BlockSpec(memory_space=pltpu.SMEM)
ALL_COLUMNS = tuple((a, b) for a in range(1, 5) for b in range(1, 5))


def run_moments(table, strips):
    return pl.pallas_call(
        moment_kernel,
        out_shape=jax.ShapeDtypeStruct((6, LOCAL, 128), F32),
        in_specs=[SMEM] + [VMEM] * 6,
        out_specs=VMEM,
        scratch_shapes=[
            pltpu.VMEM((8, TOTAL, 128), F32),
            pltpu.VMEM((TOTAL, 128, KA), BF16),
            pltpu.VMEM((LOCAL, KA, 128), BF16),
            pltpu.VMEM((TOTAL, M1, 128), BF16),
            pltpu.VMEM((10 * 64, 128), F32),
            pltpu.VMEM((M1 * 8, 128), F32),
            pltpu.VMEM((4, NB * 128, 128), F32),
            pltpu.VMEM((LOCAL * M1, 128), F32),
        ],
        compiler_params=pltpu.CompilerParams(vmem_limit_bytes=56 * 2**20),
        name="moments",
    )(table, jnp.asarray(spread_matrix(), BF16), *strips)


def run_rates(table, strips, corr_strips):
    return pl.pallas_call(
        rate_kernel,
        out_shape=(jax.ShapeDtypeStruct((LOCAL, 128), F32), jax.ShapeDtypeStruct((3, LOCAL, 128), F32)),
        in_specs=[SMEM] + [VMEM] * 11,
        out_specs=(VMEM, VMEM),
        scratch_shapes=[
            pltpu.VMEM((8, TOTAL, 128), F32),
            pltpu.VMEM((6, TOTAL, 128), F32),
            pltpu.VMEM((TOTAL, 128, KA), BF16),
            pltpu.VMEM((LOCAL, KA, 256), BF16),
            pltpu.VMEM((TOTAL, 128, 128), F32),
            pltpu.VMEM((TOTAL, M2, 128), BF16),
            pltpu.VMEM((10 * 64, 128), F32),
            pltpu.VMEM((M2 * 8, 128), F32),
            pltpu.VMEM((MW * 8, 128), F32),
            pltpu.VMEM((4, NB * 128, 256), F32),
            pltpu.VMEM((LOCAL * M2, 128), F32),
            pltpu.VMEM((LOCAL * MW, 128), F32),
        ],
        compiler_params=pltpu.CompilerParams(vmem_limit_bytes=60 * 2**20),
        name="rates",
    )(table, jnp.asarray(spread_matrix(), BF16), *strips, *corr_strips)


def exchange(first, last, axis):
    count = lax.axis_size(axis)
    odd = lax.axis_index(axis) % 2 == 1
    inner = [(i, i ^ 1) for i in range(count)]
    outer = [(i, i + 1) for i in range(1, count - 1, 2)] + [(i + 1, i) for i in range(1, count - 1, 2)]
    across = lax.ppermute(jnp.where(odd, last, first), axis, outer)
    within = lax.ppermute(jnp.where(odd, first, last), axis, inner)
    return jnp.where(odd, within, across), jnp.where(odd, across, within)


def with_halo(blocks):
    low_y, high_y = exchange(blocks[:, :, :1], blocks[:, :, -1:], "gy")

    def row(a):
        return jnp.concatenate([low_y[:, a:a + 1], blocks[:, a:a + 1], high_y[:, a:a + 1]], 2)

    low_x, high_x = exchange(row(0), row(3), "gx")
    return [t.reshape(blocks.shape[0], -1, 128) for t in (blocks, low_y, high_y, low_x, high_x)]


def body(positions, velocity, density, masses, counts):
    shape = density.shape
    live = lax.broadcasted_iota(jnp.int32, shape, 3) < counts[..., None]
    mass = jnp.where(live, masses, 0.0)
    strips = with_halo(jnp.concatenate([positions, velocity, density[None], mass[None]], 0))
    table = jnp.asarray(item_table(ALL_COLUMNS))
    corr = run_moments(table, strips)
    corr_strips = with_halo(corr.reshape((6,) + shape))
    rate, accel = run_rates(table, strips, corr_strips)
    return (rate.reshape(shape), accel.reshape((3,) + shape))


def solution(mesh):
    return jax.shard_map(
        body,
        mesh=mesh,
        in_specs=(
            P(None, "gx", "gy", None, None),
            P(None, "gx", "gy", None, None),
            P("gx", "gy", None, None),
            P("gx", "gy", None, None),
            P("gx", "gy", None),
        ),
        out_specs=(P("gx", "gy", None, None), P(None, "gx", "gy", None, None)),
        check_vma=False,
    )
```

```python
import functools
import math

import jax
import jax.numpy as jnp
import numpy as np
from jax import lax
from jax.experimental import pallas as pl
from jax.experimental.pallas import tpu as pltpu
from jax.sharding import PartitionSpec as P

KERNEL_GRAD = 105.0 / (16.0 * math.pi)
REGULAR = 0.2
STIFFNESS = 100.0 / 7.0
GRAVITY = 1.0
SOFTEN = 0.01
TINY = 1e-12
SYM_PAIRS = ((0, 0), (1, 1), (2, 2), (0, 1), (0, 2), (1, 2))
SYM_INDEX = ((0, 3, 4), (3, 1, 5), (4, 5, 2))
F32 = jnp.float32
BF16 = jnp.bfloat16
LOCAL = 64
TOTAL = 144
KA = 80
M1 = 32
M2 = 128
MW = 48
NB = 9
W_ROWS = 40
LEVEL_PAIRS = ((0, 0), (0, 1), (1, 0), (1, 1), (1, 2), (2, 1), (2, 2), (2, 3), (3, 2), (3, 3))


def column_bases():
    base = np.zeros((6, 6), np.int32)
    for a in range(6):
        for b in range(6):
            if a == 0:
                base[a, b] = 96 + b * 4
            elif a == 5:
                base[a, b] = 120 + b * 4
            elif b == 0:
                base[a, b] = 64 + (a - 1) * 4
            elif b == 5:
                base[a, b] = 80 + (a - 1) * 4
            else:
                base[a, b] = ((a - 1) * 4 + (b - 1)) * 4
    return base


def item_table(columns):
    base = column_bases()
    rows = []
    for c, d in LEVEL_PAIRS:
        for a, b in columns:
            row = [((a - 1) * 4 + (b - 1)) * 4 + c]
            for da in (-1, 0, 1):
                for db in (-1, 0, 1):
                    row.append(base[a + da, b + db] + d)
            rows.append(row)
    return np.asarray(rows, np.int32).reshape(-1)


def spread_matrix():
    out = np.zeros((32, 256), np.float32)
    for g in range(9):
        for r in range(8):
            out[(g // 3) * 8 + r, g * 8 + r] = 1.0
    for r in range(8):
        out[24 + r, 72 + r] = 1.0
    out[[6, 14, 22], 128:] = 1.0
    return out


def split3(x):
    h = x.astype(BF16).astype(F32)
    r = x - h
    m = r.astype(BF16).astype(F32)
    return h, m, r - m


def fixed_rows(rows_ref):
    rows_ref[...] = jnp.zeros_like(rows_ref)
    rows_ref[pl.ds(7 * 8, 8), :] = jnp.ones((8, 128), F32)


def pair_rows(state, corner, spread, k, with_targets, rows_ref, a_ref, b_ref, rho_ref):
    blk = pl.ds(pl.multiple_of(k * 8, 8), 8)
    x = [state[d, blk, :] - corner[d] for d in range(3)]
    v = [state[3 + d, blk, :] for d in range(3)]
    n2s = split3(x[0] * x[0] + x[1] * x[1] + x[2] * x[2])
    xvs = split3(x[0] * v[0] + x[1] * v[1] + x[2] * v[2])
    xs = [split3(t) for t in x]
    vs = [split3(t) for t in v]
    rs = split3(state[6, blk, :])

    def put(group, row, parts):
        for r, p in enumerate(parts):
            rows_ref[pl.ds((group * 8 + row + r) * 8, 8), :] = p

    def get(group, b):
        return rows_ref[pl.ds(group * 64 + b, 8, stride=8), :]

    for s in range(3):
        put(s, 0, [xs[d][s] for d in range(3)] + [vs[d][s] for d in range(3)] + [rs[s]])
    put(3, 0, n2s + xvs)
    if with_targets:
        for s in range(3):
            put(4 + s, 0, [-0.5 * xs[d][s] for d in range(3)])
            put(4 + s, 7, [0.25 * n2s[s]])
            if rho_ref is not None:
                put(7 + s, 0, [-vs[d][s] for d in range(3)] + [-xs[d][s] for d in range(3)])
                put(7 + s, 7, [xvs[s]])
        row = lax.broadcasted_iota(jnp.int32, (8, 128), 0)
        quarters = jnp.where(row < 3, 0.25, 0.0)
        ones = jnp.where((row >= 3) & (row < 6), 1.0, 0.0)
    cols = [jnp.concatenate([get(s, b) for s in range(4)], 0).T.astype(BF16) for b in range(8)]
    both = jnp.dot(jnp.concatenate(cols, 0), spread, preferred_element_type=F32)
    for b in range(8):
        rows = slice(b * 128, b * 128 + 128)
        a_ref[k * 8 + b] = both[rows, :KA].astype(BF16)
        if rho_ref is not None:
            rho_ref[k * 8 + b] = both[rows, 128:]
        if with_targets:
            r2_rows = [get(4 + s, b) for s in range(3)] * 3
            b_ref[k * 8 + b, :, :128] = jnp.concatenate(r2_rows + [quarters], 0).astype(BF16)
            if rho_ref is not None:
                vx_rows = [get(7 + s, b) for s in range(3)] * 3
                b_ref[k * 8 + b, :, 128:] = jnp.concatenate(vx_rows + [ones], 0).astype(BF16)


def gather_blocks(parts, state):
    at = 0
    for part in parts:
        for k in range(part.shape[1] // 8):
            yield part, pl.ds(k * 8, 8), pl.ds(at, 8)
            at += 8


def load_state(parts, state):
    peak = jnp.zeros((8, 128), F32)
    for part, src, dst in gather_blocks(parts, state):
        mass = part[7, src, :]
        live = mass > 0.0
        for d in range(6):
            state[d, dst, :] = jnp.where(live, part[d, src, :], 0.0)
        state[6, dst, :] = jnp.where(live, part[6, src, :], 1.0)
        state[7, dst, :] = mass
        peak = jnp.maximum(peak, mass)
    level = (lax.broadcasted_iota(jnp.int32, (8, 128), 0) % 4 + 1).astype(F32)
    return jnp.max(jnp.where(peak > 0.0, level, 1.0)).astype(jnp.int32)


def centre():
    return [(lax.axis_index("gx") * 8 + 4).astype(F32), (lax.axis_index("gy") * 8 + 4).astype(F32), 4.0]


def unfold(src, height, k, rows_ref):
    for b in range(8):
        for g in range(height // 8):
            rows = pl.ds(pl.multiple_of((k * 8 + b) * height, height) + g * 8, 8)
            rows_ref[pl.ds(g * 64 + b, 8, stride=8), :] = src[rows, :]


def store_features(rows_ref, features, at):
    for f in features:
        for piece in split3(f):
            rows_ref[pl.ds(at * 8, 8), :] = piece
            at += 1


def gather_features(rows_ref, out_ref, k, rows):
    for b in range(8):
        out_ref[k * 8 + b] = rows_ref[pl.ds(b, rows, stride=8), :].astype(BF16)


def hi_lo(x):
    hi = x.astype(BF16)
    return hi, (x - hi.astype(F32)).astype(BF16)


def falloff_cubed(s2):
    q = jnp.maximum(1.0 - s2 * lax.rsqrt(s2), 0.0)
    return q * q * q


CHUNKS = ((0, 2), (2, 4), (4, 6), (6, 8), (8, 9))


def for_items(n, width, one, rest):
    one(0, 0)
    one(1, 1)

    def step(s, carry):
        t = width * s
        for e in range(width):
            one(jnp.minimum(t + e + 2, n - 1), (e + 2) % 4)
            rest(t + e, e % 4)
        return carry

    lax.fori_loop(0, n // width, step, 0)


def moment_kernel(tab, spread_ref, local, low_y, high_y, low_x, high_x, corr, state, a_ref, b_ref, f_ref, rows_ref,
                  feat_ref, r_ref, acc):
    corner = centre()
    levels = load_state((local, low_y, high_y, low_x, high_x), state)
    n = (3 * levels - 2) * 16
    spread = spread_ref[...]
    fixed_rows(rows_ref)
    feat_ref[...] = jnp.zeros_like(feat_ref)

    def prepare(k, with_targets):
        pair_rows(state, corner, spread, k, with_targets, rows_ref, a_ref, b_ref, None)
        blk = pl.ds(pl.multiple_of(k * 8, 8), 8)
        x = [state[d, blk, :] - corner[d] for d in range(3)]
        vol = state[7, blk, :] / state[6, blk, :]
        vx = [vol * t for t in x]
        features = [vol] + vx + [vx[p] * x[q] for p, q in SYM_PAIRS]
        store_features(feat_ref, features, 0)
        gather_features(feat_ref, f_ref, k, M1)

    def first(k, carry):
        prepare(k, True)
        return carry

    def others(k, carry):
        prepare(k, False)
        return carry

    lax.fori_loop(0, LOCAL // 8, first, 0)
    lax.fori_loop(LOCAL // 8, TOTAL // 8, others, 0)
    acc[...] = jnp.zeros_like(acc)

    def one(t, p):
        for c in CHUNKS:
            lhs = jnp.concatenate([a_ref[tab[t * 10 + 1 + e]] for e in range(*c)], 0)
            rows = pl.ds(c[0] * 128, (c[1] - c[0]) * 128)
            r_ref[p, rows, :] = jnp.dot(lhs, b_ref[tab[t * 10]], preferred_element_type=F32)

    def rest(t, p):
        i = tab[t * 10]
        partner = [tab[t * 10 + 1 + e] for e in range(NB)]
        weights = []
        for c in CHUNKS:
            s2 = jnp.maximum(r_ref[p, pl.ds(c[0] * 128, (c[1] - c[0]) * 128), :], TINY)
            weights.append(jnp.concatenate(hi_lo(falloff_cubed(s2)), 1))
        lhs = jnp.concatenate([f_ref[j] for j in partner], 1)
        part = jnp.dot(lhs, jnp.concatenate(weights, 0), preferred_element_type=F32)
        acc[pl.ds(pl.multiple_of(i * M1, M1), M1), :] += part[:, :128] + part[:, 128:]

    for_items(n, 16, one, rest)

    def finish(k, carry):
        unfold(acc, M1, k, feat_ref)
        blk = pl.ds(pl.multiple_of(k * 8, 8), 8)
        x = [state[d, blk, :] - corner[d] for d in range(3)]

        def total(f):
            at = [feat_ref[pl.ds((3 * f + s) * 8, 8), :] for s in range(3)]
            return at[0] + (at[1] + at[2])

        t0 = total(0)
        t1 = [total(1 + d) for d in range(3)]
        mom = []
        for e, (p, q) in enumerate(SYM_PAIRS):
            value = (x[p] * t0 - t1[p]) * x[q] + (total(4 + e) - x[p] * t1[q])
            mom.append(KERNEL_GRAD * value)
        a, d, f = (mom[e] + REGULAR for e in range(3))
        b, c, e = mom[3:]
        cof_xx = d * f - e * e
        cof_xy = c * e - b * f
        cof_xz = b * e - c * d
        cof_yy = a * f - c * c
        cof_yz = b * c - a * e
        cof_zz = a * d - b * b
        scale = 1.0 / (a * cof_xx + b * cof_xy + c * cof_xz)
        for r, cof in enumerate((cof_xx, cof_yy, cof_zz, cof_xy, cof_xz, cof_yz)):
            corr[r, blk, :] = cof * scale
        return carry

    lax.fori_loop(0, LOCAL // 8, finish, 0)


def rate_kernel(tab, spread_ref, local, low_y, high_y, low_x, high_x, corr0, corr1, corr2, corr3, corr4, rate, accel,
                state, corr, a_ref, b_ref, rho_ref, f_ref, rows_ref, feat_ref, featw_ref, r_ref, acc, accw):
    corner = centre()
    levels = load_state((local, low_y, high_y, low_x, high_x), state)
    n = (3 * levels - 2) * 16
    spread = spread_ref[...]
    fixed_rows(rows_ref)
    feat_ref[...] = jnp.zeros_like(feat_ref)
    for part, src, dst in gather_blocks((corr0, corr1, corr2, corr3, corr4), corr):
        for d in range(6):
            corr[d, dst, :] = part[d, src, :]

    def pressure(rho):
        r2 = rho * rho
        return STIFFNESS * (r2 * r2 * r2 * rho - 1.0) / r2

    def times(sym, vec):
        return [sym[SYM_INDEX[p][0]] * vec[0] + sym[SYM_INDEX[p][1]] * vec[1] + sym[SYM_INDEX[p][2]] * vec[2]
                for p in range(3)]

    def prepare(k, with_targets):
        pair_rows(state, corner, spread, k, with_targets, rows_ref, a_ref, b_ref, rho_ref)
        blk = pl.ds(pl.multiple_of(k * 8, 8), 8)
        x = [state[d, blk, :] - corner[d] for d in range(3)]
        v = [state[3 + d, blk, :] for d in range(3)]
        rho = state[6, blk, :]
        m = state[7, blk, :]
        sym = [corr[r, blk, :] for r in range(6)]
        m_sym = [m * t for t in sym]
        m_sym_x = times(m_sym, x)
        m_sym_v = times(m_sym, v)
        prs = pressure(rho)
        mp = m * prs
        mv = [m * t for t in v]
        shared = [m] + [m * t for t in x] + m_sym + m_sym_x
        own = (mv + [mv[p] * x[q] for p in range(3) for q in range(3)] + m_sym_v
               + [v[0] * m_sym_x[0] + v[1] * m_sym_x[1] + v[2] * m_sym_x[2]]
               + [mp] + [mp * t for t in x] + [prs * t for t in m_sym] + [prs * t for t in m_sym_x])
        store_features(feat_ref, shared, 0)
        store_features(feat_ref, own, W_ROWS)
        gather_features(feat_ref, f_ref, k, M2)

    def first(k, carry):
        prepare(k, True)
        return carry

    def others(k, carry):
        prepare(k, False)
        return carry

    lax.fori_loop(0, LOCAL // 8, first, 0)
    lax.fori_loop(LOCAL // 8, TOTAL // 8, others, 0)
    acc[...] = jnp.zeros_like(acc)
    accw[...] = jnp.zeros_like(accw)

    def one(t, p):
        for c in CHUNKS:
            lhs = jnp.concatenate([a_ref[tab[t * 10 + 1 + e]] for e in range(*c)], 0)
            rows = pl.ds(c[0] * 128, (c[1] - c[0]) * 128)
            r_ref[p, rows, :] = jnp.dot(lhs, b_ref[tab[t * 10]], preferred_element_type=F32)

    def rest(t, p):
        i = tab[t * 10]
        partner = [tab[t * 10 + 1 + e] for e in range(NB)]
        rho_i = state[6, pl.ds(i, 1), :]
        weights = []
        viscous = []
        for c in CHUNKS:
            both = r_ref[p, pl.ds(c[0] * 128, (c[1] - c[0]) * 128), :]
            s2 = jnp.maximum(both[:, :128], TINY)
            fall = falloff_cubed(s2)
            weights.append(jnp.concatenate(hi_lo(fall), 1))
            rho_j = jnp.concatenate([rho_ref[partner[e]] for e in range(*c)], 0)
            bottom = (s2 + 0.25 * SOFTEN) * (rho_j + rho_i)
            w = fall * jnp.minimum(both[:, 128:], 0.0) * pltpu.reciprocal(bottom)
            viscous.append(jnp.concatenate(hi_lo(w), 1))
        lhs = jnp.concatenate([f_ref[j] for j in partner], 1)
        part = jnp.dot(lhs, jnp.concatenate(weights, 0), preferred_element_type=F32)
        acc[pl.ds(pl.multiple_of(i * M2, M2), M2), :] += part[:, :128] + part[:, 128:]
        part = jnp.dot(lhs[:MW], jnp.concatenate(viscous, 0), preferred_element_type=F32)
        accw[pl.ds(pl.multiple_of(i * MW, MW), MW), :] += part[:, :128] + part[:, 128:]

    for_items(n, 8, one, rest)

    def finish(k, carry):
        unfold(acc, M2, k, feat_ref)
        unfold(accw, MW, k, featw_ref)
        blk = pl.ds(pl.multiple_of(k * 8, 8), 8)
        x = [state[d, blk, :] - corner[d] for d in range(3)]
        v = [state[3 + d, blk, :] for d in range(3)]
        prs = pressure(state[6, blk, :])
        sym = [corr[r, blk, :] for r in range(6)]

        def total(ref, first_row, f):
            at = [ref[pl.ds((first_row + 3 * f + s) * 8, 8), :] for s in range(3)]
            return at[0] + (at[1] + at[2])

        shared = [total(feat_ref, 0, f) for f in range(13)]
        own = [total(feat_ref, W_ROWS, f) for f in range(29)]
        visc = [total(featw_ref, 0, f) for f in range(13)]
        m0, mx, mk, mkx = shared[0], shared[1:4], shared[4:10], shared[10:13]
        mv, mvx, mkv, mvkx = own[0:3], own[3:12], own[12:15], own[15]
        p0, px, pk, pkx = own[16], own[17:20], own[20:26], own[26:29]
        w0, wx, wk, wkx = visc[0], visc[1:4], visc[4:10], visc[10:13]
        vx = [[v[p] * (x[q] * m0 - mx[q]) - (mv[p] * x[q] - mvx[3 * p + q]) for q in range(3)] for p in range(3)]
        inner = jnp.zeros_like(m0)
        for p in range(3):
            for q in range(3):
                inner = inner + sym[SYM_INDEX[p][q]] * vx[p][q]
        mk_x = times(mk, x)
        for p in range(3):
            inner = inner + v[p] * (mk_x[p] - mkx[p]) - x[p] * mkv[p]
        inner = inner + mvkx
        live = state[7, blk, :] > 0.0
        rate[blk, :] = jnp.where(live, (-0.5 * KERNEL_GRAD) * inner, 0.0)
        near = [prs * (x[p] * m0 - mx[p]) + (x[p] * p0 - px[p]) - 0.25 * (x[p] * w0 - wx[p]) for p in range(3)]
        mine = times(sym, near)
        pk_x = times(pk, x)
        wk_x = times(wk, x)
        for p in range(3):
            far = prs * (mk_x[p] - mkx[p]) + (pk_x[p] - pkx[p]) - 0.25 * (wk_x[p] - wkx[p])
            pull = -GRAVITY if p == 2 else 0.0
            accel[p, blk, :] = jnp.where(live, (0.5 * KERNEL_GRAD) * (mine[p] + far) + pull, 0.0)
        return carry

    lax.fori_loop(0, LOCAL // 8, finish, 0)


VMEM = pl.BlockSpec(memory_space=pltpu.VMEM)
SMEM = pl.BlockSpec(memory_space=pltpu.SMEM)
ALL_COLUMNS = tuple((a, b) for a in range(1, 5) for b in range(1, 5))


def run_moments(table, strips):
    return pl.pallas_call(
        moment_kernel,
        out_shape=jax.ShapeDtypeStruct((6, LOCAL, 128), F32),
        in_specs=[SMEM] + [VMEM] * 6,
        out_specs=VMEM,
        scratch_shapes=[
            pltpu.VMEM((8, TOTAL, 128), F32),
            pltpu.VMEM((TOTAL, 128, KA), BF16),
            pltpu.VMEM((LOCAL, KA, 128), BF16),
            pltpu.VMEM((TOTAL, M1, 128), BF16),
            pltpu.VMEM((10 * 64, 128), F32),
            pltpu.VMEM((M1 * 8, 128), F32),
            pltpu.VMEM((4, NB * 128, 128), F32),
            pltpu.VMEM((LOCAL * M1, 128), F32),
        ],
        compiler_params=pltpu.CompilerParams(vmem_limit_bytes=56 * 2**20),
        name="moments",
    )(table, jnp.asarray(spread_matrix(), BF16), *strips)


def run_rates(table, strips, corr_strips):
    return pl.pallas_call(
        rate_kernel,
        out_shape=(jax.ShapeDtypeStruct((LOCAL, 128), F32), jax.ShapeDtypeStruct((3, LOCAL, 128), F32)),
        in_specs=[SMEM] + [VMEM] * 11,
        out_specs=(VMEM, VMEM),
        scratch_shapes=[
            pltpu.VMEM((8, TOTAL, 128), F32),
            pltpu.VMEM((6, TOTAL, 128), F32),
            pltpu.VMEM((TOTAL, 128, KA), BF16),
            pltpu.VMEM((LOCAL, KA, 256), BF16),
            pltpu.VMEM((TOTAL, 128, 128), F32),
            pltpu.VMEM((TOTAL, M2, 128), BF16),
            pltpu.VMEM((10 * 64, 128), F32),
            pltpu.VMEM((M2 * 8, 128), F32),
            pltpu.VMEM((MW * 8, 128), F32),
            pltpu.VMEM((4, NB * 128, 256), F32),
            pltpu.VMEM((LOCAL * M2, 128), F32),
            pltpu.VMEM((LOCAL * MW, 128), F32),
        ],
        compiler_params=pltpu.CompilerParams(vmem_limit_bytes=60 * 2**20),
        name="rates",
    )(table, jnp.asarray(spread_matrix(), BF16), *strips, *corr_strips)


def exchange(first, last, axis):
    count = lax.axis_size(axis)
    odd = lax.axis_index(axis) % 2 == 1
    inner = [(i, i ^ 1) for i in range(count)]
    outer = [(i, i + 1) for i in range(1, count - 1, 2)] + [(i + 1, i) for i in range(1, count - 1, 2)]
    across = lax.ppermute(jnp.where(odd, last, first), axis, outer)
    within = lax.ppermute(jnp.where(odd, first, last), axis, inner)
    return jnp.where(odd, within, across), jnp.where(odd, across, within)


def with_halo(blocks):
    low_y, high_y = exchange(blocks[:, :, :1], blocks[:, :, -1:], "gy")

    def row(a):
        return jnp.concatenate([low_y[:, a:a + 1], blocks[:, a:a + 1], high_y[:, a:a + 1]], 2)

    low_x, high_x = exchange(row(0), row(3), "gx")
    return [t.reshape(blocks.shape[0], -1, 128) for t in (blocks, low_y, high_y, low_x, high_x)]


def body(positions, velocity, density, masses, counts):
    shape = density.shape
    live = lax.broadcasted_iota(jnp.int32, shape, 3) < counts[..., None]
    mass = jnp.where(live, masses, 0.0)
    strips = with_halo(jnp.concatenate([positions, velocity, density[None], mass[None]], 0))
    table = jnp.asarray(item_table(ALL_COLUMNS))
    corr = run_moments(table, strips)
    corr_strips = with_halo(corr.reshape((6,) + shape))
    rate, accel = run_rates(table, strips, corr_strips)
    return (rate.reshape(shape), accel.reshape((3,) + shape))


def solution(mesh):
    return jax.shard_map(
        body,
        mesh=mesh,
        in_specs=(
            P(None, "gx", "gy", None, None),
            P(None, "gx", "gy", None, None),
            P("gx", "gy", None, None),
            P("gx", "gy", None, None),
            P("gx", "gy", None),
        ),
        out_specs=(P("gx", "gy", None, None), P(None, "gx", "gy", None, None)),
        check_vma=False,
    )
```

```python
import functools
import math

import jax
import jax.numpy as jnp
import numpy as np
from jax import lax
from jax.experimental import pallas as pl
from jax.experimental.pallas import tpu as pltpu
from jax.sharding import PartitionSpec as P

KERNEL_GRAD = 105.0 / (16.0 * math.pi)
REGULAR = 0.2
STIFFNESS = 100.0 / 7.0
GRAVITY = 1.0
SOFTEN = 0.01
TINY = 1e-12
SYM_PAIRS = ((0, 0), (1, 1), (2, 2), (0, 1), (0, 2), (1, 2))
SYM_INDEX = ((0, 3, 4), (3, 1, 5), (4, 5, 2))
F32 = jnp.float32
BF16 = jnp.bfloat16
LOCAL = 64
SPAN = 40
TOTAL = 4 * SPAN
ROW = 11
KA = 80
M1 = 32
M2 = 128
MW = 48
NB = 9
W_ROWS = 40
LEVEL_PAIRS = ((0, 0), (0, 1), (1, 0), (1, 1), (1, 2), (2, 1), (2, 2), (2, 3), (3, 2), (3, 3))


def column_slots():
    slot = np.zeros((6, 6), np.int32)
    for a in range(6):
        for b in range(6):
            if a == 0:
                slot[a, b] = 24 + b
            elif a == 5:
                slot[a, b] = 30 + b
            elif b == 0:
                slot[a, b] = 16 + a - 1
            elif b == 5:
                slot[a, b] = 20 + a - 1
            else:
                slot[a, b] = (a - 1) * 4 + (b - 1)
    return slot


def item_table(columns):
    slot = column_slots()
    rows = []
    for c, d in LEVEL_PAIRS:
        for a, b in columns:
            row = [c * 16 + slot[a, b]]
            for da in (-1, 0, 1):
                for db in (-1, 0, 1):
                    row.append(d * SPAN + slot[a + da, b + db])
            row.append(c * SPAN + slot[a, b])
            rows.append(row)
    return np.asarray(rows, np.int32).reshape(-1)


def spread_matrix():
    out = np.zeros((32, 256), np.float32)
    for g in range(9):
        for r in range(8):
            out[(g // 3) * 8 + r, g * 8 + r] = 1.0
    for r in range(8):
        out[24 + r, 72 + r] = 1.0
    out[[6, 14, 22], 128:] = 1.0
    return out


def split3(x):
    h = x.astype(BF16).astype(F32)
    r = x - h
    m = r.astype(BF16).astype(F32)
    return h, m, r - m


def fixed_rows(rows_ref):
    rows_ref[...] = jnp.zeros_like(rows_ref)
    rows_ref[pl.ds(7 * 8, 8), :] = jnp.ones((8, 128), F32)


def pair_rows(state, corner, spread, k, target, rows_ref, a_ref, b_ref, rho_ref):
    blk = pl.ds(pl.multiple_of(k * 8, 8), 8)
    x = [state[d, blk, :] - corner[d] for d in range(3)]
    v = [state[3 + d, blk, :] for d in range(3)]
    n2s = split3(x[0] * x[0] + x[1] * x[1] + x[2] * x[2])
    xvs = split3(x[0] * v[0] + x[1] * v[1] + x[2] * v[2])
    xs = [split3(t) for t in x]
    vs = [split3(t) for t in v]
    rs = split3(state[6, blk, :])

    def put(group, row, parts):
        for r, p in enumerate(parts):
            rows_ref[pl.ds((group * 8 + row + r) * 8, 8), :] = p

    def get(group, b):
        return rows_ref[pl.ds(group * 64 + b, 8, stride=8), :]

    for s in range(3):
        put(s, 0, [xs[d][s] for d in range(3)] + [vs[d][s] for d in range(3)] + [rs[s]])
    put(3, 0, n2s + xvs)
    if target is not None:
        for s in range(3):
            put(4 + s, 0, [-0.5 * xs[d][s] for d in range(3)])
            put(4 + s, 7, [0.25 * n2s[s]])
            if rho_ref is not None:
                put(7 + s, 0, [-vs[d][s] for d in range(3)] + [-xs[d][s] for d in range(3)])
                put(7 + s, 7, [xvs[s]])
        row = lax.broadcasted_iota(jnp.int32, (8, 128), 0)
        quarters = jnp.where(row < 3, 0.25, 0.0)
        ones = jnp.where((row >= 3) & (row < 6), 1.0, 0.0)
    cols = [jnp.concatenate([get(s, b) for s in range(4)], 0).T.astype(BF16) for b in range(8)]
    both = jnp.dot(jnp.concatenate(cols, 0), spread, preferred_element_type=F32)
    for b in range(8):
        rows = slice(b * 128, b * 128 + 128)
        a_ref[k * 8 + b] = both[rows, :KA].astype(BF16)
        if rho_ref is not None:
            rho_ref[k * 8 + b] = both[rows, 128:]
        if target is not None:
            r2_rows = [get(4 + s, b) for s in range(3)] * 3
            b_ref[target * 8 + b, :, :128] = jnp.concatenate(r2_rows + [quarters], 0).astype(BF16)
            if rho_ref is not None:
                vx_rows = [get(7 + s, b) for s in range(3)] * 3
                b_ref[target * 8 + b, :, 128:] = jnp.concatenate(vx_rows + [ones], 0).astype(BF16)


def by_level(parts):
    for level in range(4):
        at = level * SPAN
        for part in parts:
            columns = part.shape[1] // 4
            for first in range(0, columns, 8):
                width = min(8, columns - first)
                src = pl.ds(first * 4 + level, width, stride=4)
                yield part, src, pl.ds(at, width), level
                at += width


def load_state(parts, state):
    for d in range(8):
        for level in range(4):
            pad = pl.ds(level * SPAN + 36, 4)
            state[d, pad, :] = jnp.full((4, 128), 1.0 if d == 6 else 0.0, F32)
    peak = {}
    for part, src, dst, level in by_level(parts):
        mass = part[7, src, :]
        live = mass > 0.0
        for d in range(6):
            state[d, dst, :] = jnp.where(live, part[d, src, :], 0.0)
        state[6, dst, :] = jnp.where(live, part[6, src, :], 1.0)
        state[7, dst, :] = mass
        height = jnp.where(live, level + 1.0, 1.0)
        peak[height.shape] = jnp.maximum(peak[height.shape], height) if height.shape in peak else height
    tops = [jnp.max(p) for p in peak.values()]
    return functools.reduce(jnp.maximum, tops).astype(jnp.int32)


def for_chunks(levels, prepare):
    def first(q, carry):
        prepare(lax.div(q, 2) * 5 + lax.rem(q, 2), q)
        return carry

    def others(q, carry):
        prepare(lax.div(q, 3) * 5 + 2 + lax.rem(q, 3), None)
        return carry

    lax.fori_loop(0, 2 * levels, first, 0)
    lax.fori_loop(0, 3 * levels, others, 0)


def target_chunk(q):
    level, half = lax.div(q, 2), lax.rem(q, 2)
    blk = pl.ds(pl.multiple_of((level * 5 + half) * 8, 8), 8)
    return blk, pl.ds(half * 32 + level, 8, stride=4)


def centre():
    return [(lax.axis_index("gx") * 8 + 4).astype(F32), (lax.axis_index("gy") * 8 + 4).astype(F32), 4.0]


def unfold(src, height, k, rows_ref):
    for b in range(8):
        for g in range(height // 8):
            rows = pl.ds(pl.multiple_of((k * 8 + b) * height, height) + g * 8, 8)
            rows_ref[pl.ds(g * 64 + b, 8, stride=8), :] = src[rows, :]


def store_features(rows_ref, features, at):
    for f in features:
        for piece in split3(f):
            rows_ref[pl.ds(at * 8, 8), :] = piece
            at += 1


def gather_features(rows_ref, out_ref, k, rows):
    for b in range(8):
        out_ref[k * 8 + b] = rows_ref[pl.ds(b, rows, stride=8), :].astype(BF16)


def hi_lo(x):
    hi = x.astype(BF16)
    return hi, (x - hi.astype(F32)).astype(BF16)


def falloff_cubed(s2):
    q = jnp.maximum(1.0 - s2 * lax.rsqrt(s2), 0.0)
    return q * q * q


CHUNKS = ((0, 2), (2, 4), (4, 6), (6, 8), (8, 9))


def for_items(n, width, one, rest):
    one(0, 0)
    one(1, 1)

    def step(s, carry):
        t = width * s
        for e in range(width):
            one(jnp.minimum(t + e + 2, n - 1), (e + 2) % 4)
            rest(t + e, e % 4)
        return carry

    lax.fori_loop(0, n // width, step, 0)


def moment_kernel(tab, spread_ref, local, low_y, high_y, low_x, high_x, corr, state, a_ref, b_ref, f_ref, rows_ref,
                  feat_ref, r_ref, acc):
    corner = centre()
    levels = load_state((local, low_y, high_y, low_x, high_x), state)
    n = (3 * levels - 2) * 16
    spread = spread_ref[...]
    fixed_rows(rows_ref)
    feat_ref[...] = jnp.zeros_like(feat_ref)

    def prepare(k, target):
        pair_rows(state, corner, spread, k, target, rows_ref, a_ref, b_ref, None)
        blk = pl.ds(pl.multiple_of(k * 8, 8), 8)
        x = [state[d, blk, :] - corner[d] for d in range(3)]
        vol = state[7, blk, :] / state[6, blk, :]
        vx = [vol * t for t in x]
        features = [vol] + vx + [vx[p] * x[q] for p, q in SYM_PAIRS]
        store_features(feat_ref, features, 0)
        gather_features(feat_ref, f_ref, k, M1)

    for_chunks(levels, prepare)
    acc[...] = jnp.zeros_like(acc)
    corr[...] = jnp.zeros_like(corr)

    def one(t, p):
        for c in CHUNKS:
            lhs = jnp.concatenate([a_ref[tab[t * ROW + 1 + e]] for e in range(*c)], 0)
            rows = pl.ds(c[0] * 128, (c[1] - c[0]) * 128)
            r_ref[p, rows, :] = jnp.dot(lhs, b_ref[tab[t * ROW]], preferred_element_type=F32)

    def rest(t, p):
        i = tab[t * ROW]
        partner = [tab[t * ROW + 1 + e] for e in range(NB)]
        weights = []
        for c in CHUNKS:
            s2 = jnp.maximum(r_ref[p, pl.ds(c[0] * 128, (c[1] - c[0]) * 128), :], TINY)
            weights.append(jnp.concatenate(hi_lo(falloff_cubed(s2)), 1))
        lhs = jnp.concatenate([f_ref[j] for j in partner], 1)
        part = jnp.dot(lhs, jnp.concatenate(weights, 0), preferred_element_type=F32)
        acc[pl.ds(pl.multiple_of(i * M1, M1), M1), :] += part[:, :128] + part[:, 128:]

    for_items(n, 16, one, rest)

    def finish(k, carry):
        unfold(acc, M1, k, feat_ref)
        blk, out = target_chunk(k)
        x = [state[d, blk, :] - corner[d] for d in range(3)]

        def total(f):
            at = [feat_ref[pl.ds((3 * f + s) * 8, 8), :] for s in range(3)]
            return at[0] + (at[1] + at[2])

        t0 = total(0)
        t1 = [total(1 + d) for d in range(3)]
        mom = []
        for e, (p, q) in enumerate(SYM_PAIRS):
            value = (x[p] * t0 - t1[p]) * x[q] + (total(4 + e) - x[p] * t1[q])
            mom.append(KERNEL_GRAD * value)
        a, d, f = (mom[e] + REGULAR for e in range(3))
        b, c, e = mom[3:]
        cof_xx = d * f - e * e
        cof_xy = c * e - b * f
        cof_xz = b * e - c * d
        cof_yy = a * f - c * c
        cof_yz = b * c - a * e
        cof_zz = a * d - b * b
        scale = 1.0 / (a * cof_xx + b * cof_xy + c * cof_xz)
        for r, cof in enumerate((cof_xx, cof_yy, cof_zz, cof_xy, cof_xz, cof_yz)):
            corr[r, out, :] = cof * scale
        return carry

    lax.fori_loop(0, 2 * levels, finish, 0)


def rate_kernel(tab, spread_ref, local, low_y, high_y, low_x, high_x, corr0, corr1, corr2, corr3, corr4, rate, accel,
                state, corr, a_ref, b_ref, rho_ref, f_ref, rows_ref, feat_ref, featw_ref, r_ref, acc, accw):
    corner = centre()
    levels = load_state((local, low_y, high_y, low_x, high_x), state)
    n = (3 * levels - 2) * 16
    spread = spread_ref[...]
    fixed_rows(rows_ref)
    feat_ref[...] = jnp.zeros_like(feat_ref)
    for d in range(6):
        for level in range(4):
            corr[d, pl.ds(level * SPAN + 36, 4), :] = jnp.zeros((4, 128), F32)
    for part, src, dst, level in by_level((corr0, corr1, corr2, corr3, corr4)):
        for d in range(6):
            corr[d, dst, :] = part[d, src, :]

    def pressure(rho):
        r2 = rho * rho
        return STIFFNESS * (r2 * r2 * r2 * rho - 1.0) / r2

    def times(sym, vec):
        return [sym[SYM_INDEX[p][0]] * vec[0] + sym[SYM_INDEX[p][1]] * vec[1] + sym[SYM_INDEX[p][2]] * vec[2]
                for p in range(3)]

    def prepare(k, target):
        pair_rows(state, corner, spread, k, target, rows_ref, a_ref, b_ref, rho_ref)
        blk = pl.ds(pl.multiple_of(k * 8, 8), 8)
        x = [state[d, blk, :] - corner[d] for d in range(3)]
        v = [state[3 + d, blk, :] for d in range(3)]
        rho = state[6, blk, :]
        m = state[7, blk, :]
        sym = [corr[r, blk, :] for r in range(6)]
        m_sym = [m * t for t in sym]
        m_sym_x = times(m_sym, x)
        m_sym_v = times(m_sym, v)
        prs = pressure(rho)
        mp = m * prs
        mv = [m * t for t in v]
        shared = [m] + [m * t for t in x] + m_sym + m_sym_x
        own = (mv + [mv[p] * x[q] for p in range(3) for q in range(3)] + m_sym_v
               + [v[0] * m_sym_x[0] + v[1] * m_sym_x[1] + v[2] * m_sym_x[2]]
               + [mp] + [mp * t for t in x] + [prs * t for t in m_sym] + [prs * t for t in m_sym_x])
        store_features(feat_ref, shared, 0)
        store_features(feat_ref, own, W_ROWS)
        gather_features(feat_ref, f_ref, k, M2)

    for_chunks(levels, prepare)
    acc[...] = jnp.zeros_like(acc)
    rate[...] = jnp.zeros_like(rate)
    accel[...] = jnp.zeros_like(accel)
    accw[...] = jnp.zeros_like(accw)

    def one(t, p):
        for c in CHUNKS:
            lhs = jnp.concatenate([a_ref[tab[t * ROW + 1 + e]] for e in range(*c)], 0)
            rows = pl.ds(c[0] * 128, (c[1] - c[0]) * 128)
            r_ref[p, rows, :] = jnp.dot(lhs, b_ref[tab[t * ROW]], preferred_element_type=F32)

    def rest(t, p):
        i = tab[t * ROW]
        partner = [tab[t * ROW + 1 + e] for e in range(NB)]
        rho_i = state[6, pl.ds(tab[t * ROW + 10], 1), :]
        weights = []
        viscous = []
        for c in CHUNKS:
            both = r_ref[p, pl.ds(c[0] * 128, (c[1] - c[0]) * 128), :]
            s2 = jnp.maximum(both[:, :128], TINY)
            fall = falloff_cubed(s2)
            weights.append(jnp.concatenate(hi_lo(fall), 1))
            rho_j = jnp.concatenate([rho_ref[partner[e]] for e in range(*c)], 0)
            bottom = (s2 + 0.25 * SOFTEN) * (rho_j + rho_i)
            w = fall * jnp.minimum(both[:, 128:], 0.0) * pltpu.reciprocal(bottom)
            viscous.append(jnp.concatenate(hi_lo(w), 1))
        lhs = jnp.concatenate([f_ref[j] for j in partner], 1)
        part = jnp.dot(lhs, jnp.concatenate(weights, 0), preferred_element_type=F32)
        acc[pl.ds(pl.multiple_of(i * M2, M2), M2), :] += part[:, :128] + part[:, 128:]
        part = jnp.dot(lhs[:MW], jnp.concatenate(viscous, 0), preferred_element_type=F32)
        accw[pl.ds(pl.multiple_of(i * MW, MW), MW), :] += part[:, :128] + part[:, 128:]

    for_items(n, 8, one, rest)

    def finish(k, carry):
        unfold(acc, M2, k, feat_ref)
        unfold(accw, MW, k, featw_ref)
        blk, out = target_chunk(k)
        x = [state[d, blk, :] - corner[d] for d in range(3)]
        v = [state[3 + d, blk, :] for d in range(3)]
        prs = pressure(state[6, blk, :])
        sym = [corr[r, blk, :] for r in range(6)]

        def total(ref, first_row, f):
            at = [ref[pl.ds((first_row + 3 * f + s) * 8, 8), :] for s in range(3)]
            return at[0] + (at[1] + at[2])

        shared = [total(feat_ref, 0, f) for f in range(13)]
        own = [total(feat_ref, W_ROWS, f) for f in range(29)]
        visc = [total(featw_ref, 0, f) for f in range(13)]
        m0, mx, mk, mkx = shared[0], shared[1:4], shared[4:10], shared[10:13]
        mv, mvx, mkv, mvkx = own[0:3], own[3:12], own[12:15], own[15]
        p0, px, pk, pkx = own[16], own[17:20], own[20:26], own[26:29]
        w0, wx, wk, wkx = visc[0], visc[1:4], visc[4:10], visc[10:13]
        vx = [[v[p] * (x[q] * m0 - mx[q]) - (mv[p] * x[q] - mvx[3 * p + q]) for q in range(3)] for p in range(3)]
        inner = jnp.zeros_like(m0)
        for p in range(3):
            for q in range(3):
                inner = inner + sym[SYM_INDEX[p][q]] * vx[p][q]
        mk_x = times(mk, x)
        for p in range(3):
            inner = inner + v[p] * (mk_x[p] - mkx[p]) - x[p] * mkv[p]
        inner = inner + mvkx
        live = state[7, blk, :] > 0.0
        rate[out, :] = jnp.where(live, (-0.5 * KERNEL_GRAD) * inner, 0.0)
        near = [prs * (x[p] * m0 - mx[p]) + (x[p] * p0 - px[p]) - 0.25 * (x[p] * w0 - wx[p]) for p in range(3)]
        mine = times(sym, near)
        pk_x = times(pk, x)
        wk_x = times(wk, x)
        for p in range(3):
            far = prs * (mk_x[p] - mkx[p]) + (pk_x[p] - pkx[p]) - 0.25 * (wk_x[p] - wkx[p])
            pull = -GRAVITY if p == 2 else 0.0
            accel[p, out, :] = jnp.where(live, (0.5 * KERNEL_GRAD) * (mine[p] + far) + pull, 0.0)
        return carry

    lax.fori_loop(0, 2 * levels, finish, 0)


VMEM = pl.BlockSpec(memory_space=pltpu.VMEM)
SMEM = pl.BlockSpec(memory_space=pltpu.SMEM)
ALL_COLUMNS = tuple((a, b) for a in range(1, 5) for b in range(1, 5))


def run_moments(table, strips):
    return pl.pallas_call(
        moment_kernel,
        out_shape=jax.ShapeDtypeStruct((6, LOCAL, 128), F32),
        in_specs=[SMEM] + [VMEM] * 6,
        out_specs=VMEM,
        scratch_shapes=[
            pltpu.VMEM((8, TOTAL, 128), F32),
            pltpu.VMEM((TOTAL, 128, KA), BF16),
            pltpu.VMEM((LOCAL, KA, 128), BF16),
            pltpu.VMEM((TOTAL, M1, 128), BF16),
            pltpu.VMEM((10 * 64, 128), F32),
            pltpu.VMEM((M1 * 8, 128), F32),
            pltpu.VMEM((4, NB * 128, 128), F32),
            pltpu.VMEM((LOCAL * M1, 128), F32),
        ],
        compiler_params=pltpu.CompilerParams(vmem_limit_bytes=56 * 2**20),
        name="moments",
    )(table, jnp.asarray(spread_matrix(), BF16), *strips)


def run_rates(table, strips, corr_strips):
    return pl.pallas_call(
        rate_kernel,
        out_shape=(jax.ShapeDtypeStruct((LOCAL, 128), F32), jax.ShapeDtypeStruct((3, LOCAL, 128), F32)),
        in_specs=[SMEM] + [VMEM] * 11,
        out_specs=(VMEM, VMEM),
        scratch_shapes=[
            pltpu.VMEM((8, TOTAL, 128), F32),
            pltpu.VMEM((6, TOTAL, 128), F32),
            pltpu.VMEM((TOTAL, 128, KA), BF16),
            pltpu.VMEM((LOCAL, KA, 256), BF16),
            pltpu.VMEM((TOTAL, 128, 128), F32),
            pltpu.VMEM((TOTAL, M2, 128), BF16),
            pltpu.VMEM((10 * 64, 128), F32),
            pltpu.VMEM((M2 * 8, 128), F32),
            pltpu.VMEM((MW * 8, 128), F32),
            pltpu.VMEM((4, NB * 128, 256), F32),
            pltpu.VMEM((LOCAL * M2, 128), F32),
            pltpu.VMEM((LOCAL * MW, 128), F32),
        ],
        compiler_params=pltpu.CompilerParams(vmem_limit_bytes=60 * 2**20),
        name="rates",
    )(table, jnp.asarray(spread_matrix(), BF16), *strips, *corr_strips)


def exchange(first, last, axis):
    count = lax.axis_size(axis)
    odd = lax.axis_index(axis) % 2 == 1
    inner = [(i, i ^ 1) for i in range(count)]
    outer = [(i, i + 1) for i in range(1, count - 1, 2)] + [(i + 1, i) for i in range(1, count - 1, 2)]
    across = lax.ppermute(jnp.where(odd, last, first), axis, outer)
    within = lax.ppermute(jnp.where(odd, first, last), axis, inner)
    return jnp.where(odd, within, across), jnp.where(odd, across, within)


def with_halo(blocks):
    low_y, high_y = exchange(blocks[:, :, :1], blocks[:, :, -1:], "gy")

    def row(a):
        return jnp.concatenate([low_y[:, a:a + 1], blocks[:, a:a + 1], high_y[:, a:a + 1]], 2)

    low_x, high_x = exchange(row(0), row(3), "gx")
    return [t.reshape(blocks.shape[0], -1, 128) for t in (blocks, low_y, high_y, low_x, high_x)]


def body(positions, velocity, density, masses, counts):
    shape = density.shape
    live = lax.broadcasted_iota(jnp.int32, shape, 3) < counts[..., None]
    mass = jnp.where(live, masses, 0.0)
    strips = with_halo(jnp.concatenate([positions, velocity, density[None], mass[None]], 0))
    table = jnp.asarray(item_table(ALL_COLUMNS))
    corr = run_moments(table, strips)
    corr_strips = with_halo(corr.reshape((6,) + shape))
    rate, accel = run_rates(table, strips, corr_strips)
    return (rate.reshape(shape), accel.reshape((3,) + shape))


def solution(mesh):
    return jax.shard_map(
        body,
        mesh=mesh,
        in_specs=(
            P(None, "gx", "gy", None, None),
            P(None, "gx", "gy", None, None),
            P("gx", "gy", None, None),
            P("gx", "gy", None, None),
            P("gx", "gy", None),
        ),
        out_specs=(P("gx", "gy", None, None), P(None, "gx", "gy", None, None)),
        check_vma=False,
    )
```

```python
import functools
import math

import jax
import jax.numpy as jnp
import numpy as np
from jax import lax
from jax.experimental import pallas as pl
from jax.experimental.pallas import tpu as pltpu
from jax.sharding import PartitionSpec as P

KERNEL_GRAD = 105.0 / (16.0 * math.pi)
REGULAR = 0.2
STIFFNESS = 100.0 / 7.0
GRAVITY = 1.0
SOFTEN = 0.01
TINY = 1e-12
SYM_PAIRS = ((0, 0), (1, 1), (2, 2), (0, 1), (0, 2), (1, 2))
SYM_INDEX = ((0, 3, 4), (3, 1, 5), (4, 5, 2))
F32 = jnp.float32
BF16 = jnp.bfloat16
LOCAL = 64
SPAN = 40
TOTAL = 4 * SPAN
ROW = 11
KA = 80
M1 = 32
M2 = 128
MW = 48
NB = 9
W_ROWS = 40
LEVEL_PAIRS = ((0, 0), (0, 1), (1, 0), (1, 1), (1, 2), (2, 1), (2, 2), (2, 3), (3, 2), (3, 3))


def column_slots():
    slot = np.zeros((6, 6), np.int32)
    for a in range(6):
        for b in range(6):
            if a == 0:
                slot[a, b] = 24 + b
            elif a == 5:
                slot[a, b] = 30 + b
            elif b == 0:
                slot[a, b] = 16 + a - 1
            elif b == 5:
                slot[a, b] = 20 + a - 1
            else:
                slot[a, b] = (a - 1) * 4 + (b - 1)
    return slot


def item_table(columns):
    slot = column_slots()
    rows = []
    for c, d in LEVEL_PAIRS:
        for a, b in columns:
            row = [c * 16 + slot[a, b]]
            for da in (-1, 0, 1):
                for db in (-1, 0, 1):
                    row.append(d * SPAN + slot[a + da, b + db])
            row.append(c * SPAN + slot[a, b])
            rows.append(row)
    return np.asarray(rows, np.int32).reshape(-1)


def spread_matrix():
    out = np.zeros((32, 256), np.float32)
    for g in range(9):
        for r in range(8):
            out[(g // 3) * 8 + r, g * 8 + r] = 1.0
    for r in range(8):
        out[24 + r, 72 + r] = 1.0
    out[[6, 14, 22], 128:] = 1.0
    return out


def split3(x):
    h = x.astype(BF16).astype(F32)
    r = x - h
    m = r.astype(BF16).astype(F32)
    return h, m, r - m


def fixed_rows(rows_ref):
    rows_ref[...] = jnp.zeros_like(rows_ref)
    rows_ref[pl.ds(7 * 8, 8), :] = jnp.ones((8, 128), F32)


def pair_rows(state, corner, spread, k, target, rows_ref, a_ref, b_ref, rho_ref):
    blk = pl.ds(pl.multiple_of(k * 8, 8), 8)
    x = [state[d, blk, :] - corner[d] for d in range(3)]
    v = [state[3 + d, blk, :] for d in range(3)]
    n2s = split3(x[0] * x[0] + x[1] * x[1] + x[2] * x[2])
    xvs = split3(x[0] * v[0] + x[1] * v[1] + x[2] * v[2])
    xs = [split3(t) for t in x]
    vs = [split3(t) for t in v]
    rs = split3(state[6, blk, :])

    def put(group, row, parts):
        for r, p in enumerate(parts):
            rows_ref[pl.ds((group * 8 + row + r) * 8, 8), :] = p

    def get(group, b):
        return rows_ref[pl.ds(group * 64 + b, 8, stride=8), :]

    for s in range(3):
        put(s, 0, [xs[d][s] for d in range(3)] + [vs[d][s] for d in range(3)] + [rs[s]])
    put(3, 0, n2s + xvs)
    if target is not None:
        for s in range(3):
            put(4 + s, 0, [-0.5 * xs[d][s] for d in range(3)])
            put(4 + s, 7, [0.25 * n2s[s]])
            if rho_ref is not None:
                put(7 + s, 0, [-vs[d][s] for d in range(3)] + [-xs[d][s] for d in range(3)])
                put(7 + s, 7, [xvs[s]])
        row = lax.broadcasted_iota(jnp.int32, (8, 128), 0)
        quarters = jnp.where(row < 3, 0.25, 0.0)
        ones = jnp.where((row >= 3) & (row < 6), 1.0, 0.0)
    cols = [jnp.concatenate([get(s, b) for s in range(4)], 0).T.astype(BF16) for b in range(8)]
    both = jnp.dot(jnp.concatenate(cols, 0), spread, preferred_element_type=F32)
    for b in range(8):
        rows = slice(b * 128, b * 128 + 128)
        a_ref[k * 8 + b] = both[rows, :KA].astype(BF16)
        if rho_ref is not None:
            rho_ref[k * 8 + b] = both[rows, 128:]
        if target is not None:
            r2_rows = [get(4 + s, b) for s in range(3)] * 3
            b_ref[target * 8 + b, :, :128] = jnp.concatenate(r2_rows + [quarters], 0).astype(BF16)
            if rho_ref is not None:
                vx_rows = [get(7 + s, b) for s in range(3)] * 3
                b_ref[target * 8 + b, :, 128:] = jnp.concatenate(vx_rows + [ones], 0).astype(BF16)


def by_level(parts):
    for level in range(4):
        at = level * SPAN
        for part in parts:
            columns = part.shape[1] // 4
            for first in range(0, columns, 8):
                width = min(8, columns - first)
                src = pl.ds(first * 4 + level, width, stride=4)
                yield part, src, pl.ds(at, width), level
                at += width


def load_state(parts, state):
    for d in range(8):
        for level in range(4):
            pad = pl.ds(level * SPAN + 36, 4)
            state[d, pad, :] = jnp.full((4, 128), 1.0 if d == 6 else 0.0, F32)
    peak = {}
    for part, src, dst, level in by_level(parts):
        mass = part[7, src, :]
        live = mass > 0.0
        for d in range(6):
            state[d, dst, :] = jnp.where(live, part[d, src, :], 0.0)
        state[6, dst, :] = jnp.where(live, part[6, src, :], 1.0)
        state[7, dst, :] = mass
        height = jnp.where(live, level + 1.0, 1.0)
        peak[height.shape] = jnp.maximum(peak[height.shape], height) if height.shape in peak else height
    tops = [jnp.max(p) for p in peak.values()]
    return functools.reduce(jnp.maximum, tops).astype(jnp.int32)


def for_chunks(levels, prepare):
    def first(q, carry):
        prepare(lax.div(q, 2) * 5 + lax.rem(q, 2), q)
        return carry

    def others(q, carry):
        prepare(lax.div(q, 3) * 5 + 2 + lax.rem(q, 3), None)
        return carry

    lax.fori_loop(0, 2 * levels, first, 0)
    lax.fori_loop(0, 3 * levels, others, 0)


def target_chunk(q):
    level, half = lax.div(q, 2), lax.rem(q, 2)
    blk = pl.ds(pl.multiple_of((level * 5 + half) * 8, 8), 8)
    return blk, pl.ds(half * 32 + level, 8, stride=4)


def centre():
    return [(lax.axis_index("gx") * 8 + 4).astype(F32), (lax.axis_index("gy") * 8 + 4).astype(F32), 4.0]


def unfold(src, height, k, rows_ref):
    for b in range(8):
        for g in range(height // 8):
            rows = pl.ds(pl.multiple_of((k * 8 + b) * height, height) + g * 8, 8)
            rows_ref[pl.ds(g * 64 + b, 8, stride=8), :] = src[rows, :]


def store_features(rows_ref, features, at):
    for f in features:
        for piece in split3(f):
            rows_ref[pl.ds(at * 8, 8), :] = piece
            at += 1


def gather_features(rows_ref, out_ref, k, rows):
    for b in range(8):
        out_ref[k * 8 + b] = rows_ref[pl.ds(b, rows, stride=8), :].astype(BF16)


def hi_lo(x):
    hi = x.astype(BF16)
    return hi, (x - hi.astype(F32)).astype(BF16)


def falloff_cubed(s2):
    q = jnp.maximum(1.0 - s2 * lax.rsqrt(s2), 0.0)
    return q * q * q


CHUNKS = ((0, NB),)


def for_items(n, width, one, rest):
    one(0, 0)
    one(1, 1)

    def step(s, carry):
        t = width * s
        for e in range(width):
            one(jnp.minimum(t + e + 2, n - 1), (e + 2) % 4)
            rest(t + e, e % 4)
        return carry

    lax.fori_loop(0, n // width, step, 0)


def moment_kernel(tab, spread_ref, local, low_y, high_y, low_x, high_x, corr, state, a_ref, b_ref, f_ref, rows_ref,
                  feat_ref, r_ref, acc):
    corner = centre()
    levels = load_state((local, low_y, high_y, low_x, high_x), state)
    n = (3 * levels - 2) * 16
    spread = spread_ref[...]
    fixed_rows(rows_ref)
    feat_ref[...] = jnp.zeros_like(feat_ref)

    def prepare(k, target):
        pair_rows(state, corner, spread, k, target, rows_ref, a_ref, b_ref, None)
        blk = pl.ds(pl.multiple_of(k * 8, 8), 8)
        x = [state[d, blk, :] - corner[d] for d in range(3)]
        vol = state[7, blk, :] / state[6, blk, :]
        vx = [vol * t for t in x]
        features = [vol] + vx + [vx[p] * x[q] for p, q in SYM_PAIRS]
        store_features(feat_ref, features, 0)
        gather_features(feat_ref, f_ref, k, M1)

    for_chunks(levels, prepare)
    acc[...] = jnp.zeros_like(acc)
    corr[...] = jnp.zeros_like(corr)

    def one(t, p):
        for c in CHUNKS:
            lhs = jnp.concatenate([a_ref[tab[t * ROW + 1 + e]] for e in range(*c)], 0)
            rows = pl.ds(c[0] * 128, (c[1] - c[0]) * 128)
            r_ref[p, rows, :] = jnp.dot(lhs, b_ref[tab[t * ROW]], preferred_element_type=F32)

    def rest(t, p):
        i = tab[t * ROW]
        partner = [tab[t * ROW + 1 + e] for e in range(NB)]
        weights = []
        for c in CHUNKS:
            s2 = jnp.maximum(r_ref[p, pl.ds(c[0] * 128, (c[1] - c[0]) * 128), :], TINY)
            weights.append(jnp.concatenate(hi_lo(falloff_cubed(s2)), 1))
        lhs = jnp.concatenate([f_ref[j] for j in partner], 1)
        part = jnp.dot(lhs, jnp.concatenate(weights, 0), preferred_element_type=F32)
        acc[pl.ds(pl.multiple_of(i * M1, M1), M1), :] += part[:, :128] + part[:, 128:]

    for_items(n, 16, one, rest)

    def finish(k, carry):
        unfold(acc, M1, k, feat_ref)
        blk, out = target_chunk(k)
        x = [state[d, blk, :] - corner[d] for d in range(3)]

        def total(f):
            at = [feat_ref[pl.ds((3 * f + s) * 8, 8), :] for s in range(3)]
            return at[0] + (at[1] + at[2])

        t0 = total(0)
        t1 = [total(1 + d) for d in range(3)]
        mom = []
        for e, (p, q) in enumerate(SYM_PAIRS):
            value = (x[p] * t0 - t1[p]) * x[q] + (total(4 + e) - x[p] * t1[q])
            mom.append(KERNEL_GRAD * value)
        a, d, f = (mom[e] + REGULAR for e in range(3))
        b, c, e = mom[3:]
        cof_xx = d * f - e * e
        cof_xy = c * e - b * f
        cof_xz = b * e - c * d
        cof_yy = a * f - c * c
        cof_yz = b * c - a * e
        cof_zz = a * d - b * b
        scale = 1.0 / (a * cof_xx + b * cof_xy + c * cof_xz)
        for r, cof in enumerate((cof_xx, cof_yy, cof_zz, cof_xy, cof_xz, cof_yz)):
            corr[r, out, :] = cof * scale
        return carry

    lax.fori_loop(0, 2 * levels, finish, 0)


def rate_kernel(tab, spread_ref, local, low_y, high_y, low_x, high_x, corr0, corr1, corr2, corr3, corr4, rate, accel,
                state, corr, a_ref, b_ref, rho_ref, f_ref, rows_ref, feat_ref, featw_ref, r_ref, acc, accw):
    corner = centre()
    levels = load_state((local, low_y, high_y, low_x, high_x), state)
    n = (3 * levels - 2) * 16
    spread = spread_ref[...]
    fixed_rows(rows_ref)
    feat_ref[...] = jnp.zeros_like(feat_ref)
    for d in range(6):
        for level in range(4):
            corr[d, pl.ds(level * SPAN + 36, 4), :] = jnp.zeros((4, 128), F32)
    for part, src, dst, level in by_level((corr0, corr1, corr2, corr3, corr4)):
        for d in range(6):
            corr[d, dst, :] = part[d, src, :]

    def pressure(rho):
        r2 = rho * rho
        return STIFFNESS * (r2 * r2 * r2 * rho - 1.0) / r2

    def times(sym, vec):
        return [sym[SYM_INDEX[p][0]] * vec[0] + sym[SYM_INDEX[p][1]] * vec[1] + sym[SYM_INDEX[p][2]] * vec[2]
                for p in range(3)]

    def prepare(k, target):
        pair_rows(state, corner, spread, k, target, rows_ref, a_ref, b_ref, rho_ref)
        blk = pl.ds(pl.multiple_of(k * 8, 8), 8)
        x = [state[d, blk, :] - corner[d] for d in range(3)]
        v = [state[3 + d, blk, :] for d in range(3)]
        rho = state[6, blk, :]
        m = state[7, blk, :]
        sym = [corr[r, blk, :] for r in range(6)]
        m_sym = [m * t for t in sym]
        m_sym_x = times(m_sym, x)
        m_sym_v = times(m_sym, v)
        prs = pressure(rho)
        mp = m * prs
        mv = [m * t for t in v]
        shared = [m] + [m * t for t in x] + m_sym + m_sym_x
        own = (mv + [mv[p] * x[q] for p in range(3) for q in range(3)] + m_sym_v
               + [v[0] * m_sym_x[0] + v[1] * m_sym_x[1] + v[2] * m_sym_x[2]]
               + [mp] + [mp * t for t in x] + [prs * t for t in m_sym] + [prs * t for t in m_sym_x])
        store_features(feat_ref, shared, 0)
        store_features(feat_ref, own, W_ROWS)
        gather_features(feat_ref, f_ref, k, M2)

    for_chunks(levels, prepare)
    acc[...] = jnp.zeros_like(acc)
    rate[...] = jnp.zeros_like(rate)
    accel[...] = jnp.zeros_like(accel)
    accw[...] = jnp.zeros_like(accw)

    def one(t, p):
        for c in CHUNKS:
            lhs = jnp.concatenate([a_ref[tab[t * ROW + 1 + e]] for e in range(*c)], 0)
            rows = pl.ds(c[0] * 128, (c[1] - c[0]) * 128)
            r_ref[p, rows, :] = jnp.dot(lhs, b_ref[tab[t * ROW]], preferred_element_type=F32)

    def rest(t, p):
        i = tab[t * ROW]
        partner = [tab[t * ROW + 1 + e] for e in range(NB)]
        rho_i = state[6, pl.ds(tab[t * ROW + 10], 1), :]
        weights = []
        viscous = []
        for c in CHUNKS:
            both = r_ref[p, pl.ds(c[0] * 128, (c[1] - c[0]) * 128), :]
            s2 = jnp.maximum(both[:, :128], TINY)
            fall = falloff_cubed(s2)
            weights.append(jnp.concatenate(hi_lo(fall), 1))
            rho_j = jnp.concatenate([rho_ref[partner[e]] for e in range(*c)], 0)
            bottom = (s2 + 0.25 * SOFTEN) * (rho_j + rho_i)
            w = fall * jnp.minimum(both[:, 128:], 0.0) * pltpu.reciprocal(bottom)
            viscous.append(jnp.concatenate(hi_lo(w), 1))
        lhs = jnp.concatenate([f_ref[j] for j in partner], 1)
        part = jnp.dot(lhs, jnp.concatenate(weights, 0), preferred_element_type=F32)
        acc[pl.ds(pl.multiple_of(i * M2, M2), M2), :] += part[:, :128] + part[:, 128:]
        part = jnp.dot(lhs[:MW], jnp.concatenate(viscous, 0), preferred_element_type=F32)
        accw[pl.ds(pl.multiple_of(i * MW, MW), MW), :] += part[:, :128] + part[:, 128:]

    for_items(n, 8, one, rest)

    def finish(k, carry):
        unfold(acc, M2, k, feat_ref)
        unfold(accw, MW, k, featw_ref)
        blk, out = target_chunk(k)
        x = [state[d, blk, :] - corner[d] for d in range(3)]
        v = [state[3 + d, blk, :] for d in range(3)]
        prs = pressure(state[6, blk, :])
        sym = [corr[r, blk, :] for r in range(6)]

        def total(ref, first_row, f):
            at = [ref[pl.ds((first_row + 3 * f + s) * 8, 8), :] for s in range(3)]
            return at[0] + (at[1] + at[2])

        shared = [total(feat_ref, 0, f) for f in range(13)]
        own = [total(feat_ref, W_ROWS, f) for f in range(29)]
        visc = [total(featw_ref, 0, f) for f in range(13)]
        m0, mx, mk, mkx = shared[0], shared[1:4], shared[4:10], shared[10:13]
        mv, mvx, mkv, mvkx = own[0:3], own[3:12], own[12:15], own[15]
        p0, px, pk, pkx = own[16], own[17:20], own[20:26], own[26:29]
        w0, wx, wk, wkx = visc[0], visc[1:4], visc[4:10], visc[10:13]
        vx = [[v[p] * (x[q] * m0 - mx[q]) - (mv[p] * x[q] - mvx[3 * p + q]) for q in range(3)] for p in range(3)]
        inner = jnp.zeros_like(m0)
        for p in range(3):
            for q in range(3):
                inner = inner + sym[SYM_INDEX[p][q]] * vx[p][q]
        mk_x = times(mk, x)
        for p in range(3):
            inner = inner + v[p] * (mk_x[p] - mkx[p]) - x[p] * mkv[p]
        inner = inner + mvkx
        live = state[7, blk, :] > 0.0
        rate[out, :] = jnp.where(live, (-0.5 * KERNEL_GRAD) * inner, 0.0)
        near = [prs * (x[p] * m0 - mx[p]) + (x[p] * p0 - px[p]) - 0.25 * (x[p] * w0 - wx[p]) for p in range(3)]
        mine = times(sym, near)
        pk_x = times(pk, x)
        wk_x = times(wk, x)
        for p in range(3):
            far = prs * (mk_x[p] - mkx[p]) + (pk_x[p] - pkx[p]) - 0.25 * (wk_x[p] - wkx[p])
            pull = -GRAVITY if p == 2 else 0.0
            accel[p, out, :] = jnp.where(live, (0.5 * KERNEL_GRAD) * (mine[p] + far) + pull, 0.0)
        return carry

    lax.fori_loop(0, 2 * levels, finish, 0)


VMEM = pl.BlockSpec(memory_space=pltpu.VMEM)
SMEM = pl.BlockSpec(memory_space=pltpu.SMEM)
ALL_COLUMNS = tuple((a, b) for a in range(1, 5) for b in range(1, 5))


def run_moments(table, strips):
    return pl.pallas_call(
        moment_kernel,
        out_shape=jax.ShapeDtypeStruct((6, LOCAL, 128), F32),
        in_specs=[SMEM] + [VMEM] * 6,
        out_specs=VMEM,
        scratch_shapes=[
            pltpu.VMEM((8, TOTAL, 128), F32),
            pltpu.VMEM((TOTAL, 128, KA), BF16),
            pltpu.VMEM((LOCAL, KA, 128), BF16),
            pltpu.VMEM((TOTAL, M1, 128), BF16),
            pltpu.VMEM((10 * 64, 128), F32),
            pltpu.VMEM((M1 * 8, 128), F32),
            pltpu.VMEM((4, NB * 128, 128), F32),
            pltpu.VMEM((LOCAL * M1, 128), F32),
        ],
        compiler_params=pltpu.CompilerParams(vmem_limit_bytes=56 * 2**20),
        name="moments",
    )(table, jnp.asarray(spread_matrix(), BF16), *strips)


def run_rates(table, strips, corr_strips):
    return pl.pallas_call(
        rate_kernel,
        out_shape=(jax.ShapeDtypeStruct((LOCAL, 128), F32), jax.ShapeDtypeStruct((3, LOCAL, 128), F32)),
        in_specs=[SMEM] + [VMEM] * 11,
        out_specs=(VMEM, VMEM),
        scratch_shapes=[
            pltpu.VMEM((8, TOTAL, 128), F32),
            pltpu.VMEM((6, TOTAL, 128), F32),
            pltpu.VMEM((TOTAL, 128, KA), BF16),
            pltpu.VMEM((LOCAL, KA, 256), BF16),
            pltpu.VMEM((TOTAL, 128, 128), F32),
            pltpu.VMEM((TOTAL, M2, 128), BF16),
            pltpu.VMEM((10 * 64, 128), F32),
            pltpu.VMEM((M2 * 8, 128), F32),
            pltpu.VMEM((MW * 8, 128), F32),
            pltpu.VMEM((4, NB * 128, 256), F32),
            pltpu.VMEM((LOCAL * M2, 128), F32),
            pltpu.VMEM((LOCAL * MW, 128), F32),
        ],
        compiler_params=pltpu.CompilerParams(vmem_limit_bytes=60 * 2**20),
        name="rates",
    )(table, jnp.asarray(spread_matrix(), BF16), *strips, *corr_strips)


def exchange(first, last, axis):
    count = lax.axis_size(axis)
    odd = lax.axis_index(axis) % 2 == 1
    inner = [(i, i ^ 1) for i in range(count)]
    outer = [(i, i + 1) for i in range(1, count - 1, 2)] + [(i + 1, i) for i in range(1, count - 1, 2)]
    across = lax.ppermute(jnp.where(odd, last, first), axis, outer)
    within = lax.ppermute(jnp.where(odd, first, last), axis, inner)
    return jnp.where(odd, within, across), jnp.where(odd, across, within)


def with_halo(blocks):
    low_y, high_y = exchange(blocks[:, :, :1], blocks[:, :, -1:], "gy")

    def row(a):
        return jnp.concatenate([low_y[:, a:a + 1], blocks[:, a:a + 1], high_y[:, a:a + 1]], 2)

    low_x, high_x = exchange(row(0), row(3), "gx")
    return [t.reshape(blocks.shape[0], -1, 128) for t in (blocks, low_y, high_y, low_x, high_x)]


def body(positions, velocity, density, masses, counts):
    shape = density.shape
    live = lax.broadcasted_iota(jnp.int32, shape, 3) < counts[..., None]
    mass = jnp.where(live, masses, 0.0)
    strips = with_halo(jnp.concatenate([positions, velocity, density[None], mass[None]], 0))
    table = jnp.asarray(item_table(ALL_COLUMNS))
    corr = run_moments(table, strips)
    corr_strips = with_halo(corr.reshape((6,) + shape))
    rate, accel = run_rates(table, strips, corr_strips)
    return (rate.reshape(shape), accel.reshape((3,) + shape))


def solution(mesh):
    return jax.shard_map(
        body,
        mesh=mesh,
        in_specs=(
            P(None, "gx", "gy", None, None),
            P(None, "gx", "gy", None, None),
            P("gx", "gy", None, None),
            P("gx", "gy", None, None),
            P("gx", "gy", None),
        ),
        out_specs=(P("gx", "gy", None, None), P(None, "gx", "gy", None, None)),
        check_vma=False,
    )
```

```python
import functools
import math

import jax
import jax.numpy as jnp
import numpy as np
from jax import lax
from jax.experimental import pallas as pl
from jax.experimental.pallas import tpu as pltpu
from jax.sharding import PartitionSpec as P

KERNEL_GRAD = 105.0 / (16.0 * math.pi)
REGULAR = 0.2
STIFFNESS = 100.0 / 7.0
GRAVITY = 1.0
SOFTEN = 0.01
TINY = 1e-12
SYM_PAIRS = ((0, 0), (1, 1), (2, 2), (0, 1), (0, 2), (1, 2))
SYM_INDEX = ((0, 3, 4), (3, 1, 5), (4, 5, 2))
F32 = jnp.float32
BF16 = jnp.bfloat16
LOCAL = 64
SPAN = 40
TOTAL = 4 * SPAN
ROW = 11
KA = 80
M1 = 32
M2 = 128
MW = 48
NB = 9
W_ROWS = 40
LEVEL_PAIRS = ((0, 0), (0, 1), (1, 0), (1, 1), (1, 2), (2, 1), (2, 2), (2, 3), (3, 2), (3, 3))


def column_slots():
    slot = np.zeros((6, 6), np.int32)
    for a in range(6):
        for b in range(6):
            if a == 0:
                slot[a, b] = 24 + b
            elif a == 5:
                slot[a, b] = 30 + b
            elif b == 0:
                slot[a, b] = 16 + a - 1
            elif b == 5:
                slot[a, b] = 20 + a - 1
            else:
                slot[a, b] = (a - 1) * 4 + (b - 1)
    return slot


def item_table(columns):
    slot = column_slots()
    rows = []
    for c, d in LEVEL_PAIRS:
        for a, b in columns:
            row = [c * 16 + slot[a, b]]
            for da in (-1, 0, 1):
                for db in (-1, 0, 1):
                    row.append(d * SPAN + slot[a + da, b + db])
            row.append(c * SPAN + slot[a, b])
            rows.append(row)
    return np.asarray(rows, np.int32).reshape(-1)


def spread_matrix():
    out = np.zeros((32, 256), np.float32)
    for g in range(9):
        for r in range(8):
            out[(g // 3) * 8 + r, g * 8 + r] = 1.0
    for r in range(8):
        out[24 + r, 72 + r] = 1.0
    out[[6, 14, 22], 128:] = 1.0
    return out


def split3(x):
    h = x.astype(BF16).astype(F32)
    r = x - h
    m = r.astype(BF16).astype(F32)
    return h, m, r - m


def fixed_rows(rows_ref):
    rows_ref[...] = jnp.zeros_like(rows_ref)
    rows_ref[pl.ds(7 * 8, 8), :] = jnp.ones((8, 128), F32)


def pair_rows(state, corner, spread, k, target, rows_ref, a_ref, b_ref, rho_ref):
    blk = pl.ds(pl.multiple_of(k * 8, 8), 8)
    x = [state[d, blk, :] - corner[d] for d in range(3)]
    v = [state[3 + d, blk, :] for d in range(3)]
    n2s = split3(x[0] * x[0] + x[1] * x[1] + x[2] * x[2])
    xvs = split3(x[0] * v[0] + x[1] * v[1] + x[2] * v[2])
    xs = [split3(t) for t in x]
    vs = [split3(t) for t in v]
    rs = split3(state[6, blk, :])

    def put(group, row, parts):
        for r, p in enumerate(parts):
            rows_ref[pl.ds((group * 8 + row + r) * 8, 8), :] = p

    def get(group, b):
        return rows_ref[pl.ds(group * 64 + b, 8, stride=8), :]

    for s in range(3):
        put(s, 0, [xs[d][s] for d in range(3)] + [vs[d][s] for d in range(3)] + [rs[s]])
    put(3, 0, n2s + xvs)
    if target is not None:
        for s in range(3):
            put(4 + s, 0, [-0.5 * xs[d][s] for d in range(3)])
            put(4 + s, 7, [0.25 * n2s[s]])
            if rho_ref is not None:
                put(7 + s, 0, [-vs[d][s] for d in range(3)] + [-xs[d][s] for d in range(3)])
                put(7 + s, 7, [xvs[s]])
        row = lax.broadcasted_iota(jnp.int32, (8, 128), 0)
        quarters = jnp.where(row < 3, 0.25, 0.0)
        ones = jnp.where((row >= 3) & (row < 6), 1.0, 0.0)
    cols = [jnp.concatenate([get(s, b) for s in range(4)], 0).T.astype(BF16) for b in range(8)]
    both = jnp.dot(jnp.concatenate(cols, 0), spread, preferred_element_type=F32)
    for b in range(8):
        rows = slice(b * 128, b * 128 + 128)
        a_ref[k * 8 + b] = both[rows, :KA].astype(BF16)
        if rho_ref is not None:
            rho_ref[k * 8 + b] = both[rows, 128:]
        if target is not None:
            r2_rows = [get(4 + s, b) for s in range(3)] * 3
            b_ref[target * 8 + b, :, :128] = jnp.concatenate(r2_rows + [quarters], 0).astype(BF16)
            if rho_ref is not None:
                vx_rows = [get(7 + s, b) for s in range(3)] * 3
                b_ref[target * 8 + b, :, 128:] = jnp.concatenate(vx_rows + [ones], 0).astype(BF16)


def by_level(parts):
    for level in range(4):
        at = level * SPAN
        for part in parts:
            columns = part.shape[1] // 4
            for first in range(0, columns, 8):
                width = min(8, columns - first)
                src = pl.ds(first * 4 + level, width, stride=4)
                yield part, src, pl.ds(at, width), level
                at += width


def load_state(parts, state):
    for d in range(8):
        for level in range(4):
            pad = pl.ds(level * SPAN + 36, 4)
            state[d, pad, :] = jnp.full((4, 128), 1.0 if d == 6 else 0.0, F32)
    peak = {}
    for part, src, dst, level in by_level(parts):
        mass = part[7, src, :]
        live = mass > 0.0
        for d in range(6):
            state[d, dst, :] = jnp.where(live, part[d, src, :], 0.0)
        state[6, dst, :] = jnp.where(live, part[6, src, :], 1.0)
        state[7, dst, :] = mass
        height = jnp.where(live, level + 1.0, 1.0)
        peak[height.shape] = jnp.maximum(peak[height.shape], height) if height.shape in peak else height
    tops = [jnp.max(p) for p in peak.values()]
    return functools.reduce(jnp.maximum, tops).astype(jnp.int32)


def for_chunks(levels, prepare):
    def first(q, carry):
        prepare(lax.div(q, 2) * 5 + lax.rem(q, 2), q)
        return carry

    def others(q, carry):
        prepare(lax.div(q, 3) * 5 + 2 + lax.rem(q, 3), None)
        return carry

    lax.fori_loop(0, 2 * levels, first, 0)
    lax.fori_loop(0, 3 * levels, others, 0)


def target_chunk(q):
    level, half = lax.div(q, 2), lax.rem(q, 2)
    blk = pl.ds(pl.multiple_of((level * 5 + half) * 8, 8), 8)
    return blk, pl.ds(half * 32 + level, 8, stride=4)


def centre():
    return [(lax.axis_index("gx") * 8 + 4).astype(F32), (lax.axis_index("gy") * 8 + 4).astype(F32), 4.0]


def unfold(src, height, k, rows_ref):
    for b in range(8):
        for g in range(height // 8):
            rows = pl.ds(pl.multiple_of((k * 8 + b) * height, height) + g * 8, 8)
            rows_ref[pl.ds(g * 64 + b, 8, stride=8), :] = src[rows, :]


def store_features(rows_ref, features, at):
    for f in features:
        for piece in split3(f):
            rows_ref[pl.ds(at * 8, 8), :] = piece
            at += 1


def gather_features(rows_ref, out_ref, k, rows):
    for b in range(8):
        out_ref[k * 8 + b] = rows_ref[pl.ds(b, rows, stride=8), :].astype(BF16)


def hi_lo(x):
    hi = x.astype(BF16)
    return hi, (x - hi.astype(F32)).astype(BF16)


def falloff_cubed(s2):
    q = jnp.maximum(1.0 - s2 * lax.rsqrt(s2), 0.0)
    return q * q * q


CHUNKS = ((0, NB),)


def for_items(n, width, one, rest):
    one(0, 0)
    one(1, 1)

    def step(s, carry):
        t = width * s
        for e in range(width):
            one(jnp.minimum(t + e + 2, n - 1), (e + 2) % 4)
            rest(t + e, e % 4)
        return carry

    lax.fori_loop(0, n // width, step, 0)


def moment_kernel(tab, spread_ref, local, low_y, high_y, low_x, high_x, corr, state, a_ref, b_ref, f_ref, rows_ref,
                  feat_ref, r_ref, acc):
    corner = centre()
    levels = load_state((local, low_y, high_y, low_x, high_x), state)
    n = (3 * levels - 2) * 16
    spread = spread_ref[...]
    fixed_rows(rows_ref)
    feat_ref[...] = jnp.zeros_like(feat_ref)

    def prepare(k, target):
        pair_rows(state, corner, spread, k, target, rows_ref, a_ref, b_ref, None)
        blk = pl.ds(pl.multiple_of(k * 8, 8), 8)
        x = [state[d, blk, :] - corner[d] for d in range(3)]
        vol = state[7, blk, :] / state[6, blk, :]
        vx = [vol * t for t in x]
        features = [vol] + vx + [vx[p] * x[q] for p, q in SYM_PAIRS]
        store_features(feat_ref, features, 0)
        gather_features(feat_ref, f_ref, k, M1)

    for_chunks(levels, prepare)
    acc[...] = jnp.zeros_like(acc)
    corr[...] = jnp.zeros_like(corr)

    def one(t, p):
        for c in CHUNKS:
            lhs = jnp.concatenate([a_ref[tab[t * ROW + 1 + e]] for e in range(*c)], 0)
            rows = pl.ds(c[0] * 128, (c[1] - c[0]) * 128)
            r_ref[p, rows, :] = jnp.dot(lhs, b_ref[tab[t * ROW]], preferred_element_type=F32)

    def rest(t, p):
        i = tab[t * ROW]
        partner = [tab[t * ROW + 1 + e] for e in range(NB)]
        weights = []
        for c in CHUNKS:
            s2 = jnp.maximum(r_ref[p, pl.ds(c[0] * 128, (c[1] - c[0]) * 128), :], TINY)
            weights.append(jnp.concatenate(hi_lo(falloff_cubed(s2)), 1))
        lhs = jnp.concatenate([f_ref[j] for j in partner], 1)
        part = jnp.dot(lhs, jnp.concatenate(weights, 0), preferred_element_type=F32)
        acc[pl.ds(pl.multiple_of(i * M1, M1), M1), :] += part[:, :128] + part[:, 128:]

    for_items(n, 16, one, rest)

    def finish(k, carry):
        unfold(acc, M1, k, feat_ref)
        blk, out = target_chunk(k)
        x = [state[d, blk, :] - corner[d] for d in range(3)]

        def total(f):
            at = [feat_ref[pl.ds((3 * f + s) * 8, 8), :] for s in range(3)]
            return at[0] + (at[1] + at[2])

        t0 = total(0)
        t1 = [total(1 + d) for d in range(3)]
        mom = []
        for e, (p, q) in enumerate(SYM_PAIRS):
            value = (x[p] * t0 - t1[p]) * x[q] + (total(4 + e) - x[p] * t1[q])
            mom.append(KERNEL_GRAD * value)
        a, d, f = (mom[e] + REGULAR for e in range(3))
        b, c, e = mom[3:]
        cof_xx = d * f - e * e
        cof_xy = c * e - b * f
        cof_xz = b * e - c * d
        cof_yy = a * f - c * c
        cof_yz = b * c - a * e
        cof_zz = a * d - b * b
        scale = 1.0 / (a * cof_xx + b * cof_xy + c * cof_xz)
        for r, cof in enumerate((cof_xx, cof_yy, cof_zz, cof_xy, cof_xz, cof_yz)):
            corr[r, out, :] = cof * scale
        return carry

    lax.fori_loop(0, 2 * levels, finish, 0)


def rate_kernel(tab, spread_ref, local, low_y, high_y, low_x, high_x, corr0, corr1, corr2, corr3, corr4, rate, accel,
                state, corr, a_ref, b_ref, rho_ref, f_ref, rows_ref, feat_ref, featw_ref, r_ref, acc, accw):
    corner = centre()
    levels = load_state((local, low_y, high_y, low_x, high_x), state)
    n = (3 * levels - 2) * 16
    spread = spread_ref[...]
    fixed_rows(rows_ref)
    feat_ref[...] = jnp.zeros_like(feat_ref)
    for d in range(6):
        for level in range(4):
            corr[d, pl.ds(level * SPAN + 36, 4), :] = jnp.zeros((4, 128), F32)
    for part, src, dst, level in by_level((corr0, corr1, corr2, corr3, corr4)):
        for d in range(6):
            corr[d, dst, :] = part[d, src, :]

    def pressure(rho):
        r2 = rho * rho
        return STIFFNESS * (r2 * r2 * r2 * rho - 1.0) / r2

    def times(sym, vec):
        return [sym[SYM_INDEX[p][0]] * vec[0] + sym[SYM_INDEX[p][1]] * vec[1] + sym[SYM_INDEX[p][2]] * vec[2]
                for p in range(3)]

    def prepare(k, target):
        pair_rows(state, corner, spread, k, target, rows_ref, a_ref, b_ref, rho_ref)
        blk = pl.ds(pl.multiple_of(k * 8, 8), 8)
        x = [state[d, blk, :] - corner[d] for d in range(3)]
        v = [state[3 + d, blk, :] for d in range(3)]
        rho = state[6, blk, :]
        m = state[7, blk, :]
        sym = [corr[r, blk, :] for r in range(6)]
        m_sym = [m * t for t in sym]
        m_sym_x = times(m_sym, x)
        m_sym_v = times(m_sym, v)
        prs = pressure(rho)
        mp = m * prs
        mv = [m * t for t in v]
        shared = [m] + [m * t for t in x] + m_sym + m_sym_x
        own = (mv + [mv[p] * x[q] for p in range(3) for q in range(3)] + m_sym_v
               + [v[0] * m_sym_x[0] + v[1] * m_sym_x[1] + v[2] * m_sym_x[2]]
               + [mp] + [mp * t for t in x] + [prs * t for t in m_sym] + [prs * t for t in m_sym_x])
        store_features(feat_ref, shared, 0)
        store_features(feat_ref, own, W_ROWS)
        gather_features(feat_ref, f_ref, k, M2)

    for_chunks(levels, prepare)
    acc[...] = jnp.zeros_like(acc)
    rate[...] = jnp.zeros_like(rate)
    accel[...] = jnp.zeros_like(accel)
    accw[...] = jnp.zeros_like(accw)

    def one(t, p):
        for c in CHUNKS:
            lhs = jnp.concatenate([a_ref[tab[t * ROW + 1 + e]] for e in range(*c)], 0)
            rows = pl.ds(c[0] * 128, (c[1] - c[0]) * 128)
            r_ref[p, rows, :] = jnp.dot(lhs, b_ref[tab[t * ROW]], preferred_element_type=F32)

    def rest(t, p):
        i = tab[t * ROW]
        partner = [tab[t * ROW + 1 + e] for e in range(NB)]
        rho_i = state[6, pl.ds(tab[t * ROW + 10], 1), :]
        weights = []
        viscous = []
        for c in CHUNKS:
            both = r_ref[p, pl.ds(c[0] * 128, (c[1] - c[0]) * 128), :]
            s2 = jnp.maximum(both[:, :128], TINY)
            fall = falloff_cubed(s2)
            weights.append(jnp.concatenate(hi_lo(fall), 1))
            rho_j = jnp.concatenate([rho_ref[partner[e]] for e in range(*c)], 0)
            bottom = (s2 + 0.25 * SOFTEN) * (rho_j + rho_i)
            w = fall * jnp.minimum(both[:, 128:], 0.0) * pltpu.reciprocal(bottom)
            viscous.append(jnp.concatenate(hi_lo(w), 1))
        lhs = jnp.concatenate([f_ref[j] for j in partner], 1)
        part = jnp.dot(lhs, jnp.concatenate(weights, 0), preferred_element_type=F32)
        acc[pl.ds(pl.multiple_of(i * M2, M2), M2), :] += part[:, :128] + part[:, 128:]
        part = jnp.dot(lhs[:MW], jnp.concatenate(viscous, 0), preferred_element_type=F32)
        accw[pl.ds(pl.multiple_of(i * MW, MW), MW), :] += part[:, :128] + part[:, 128:]

    for_items(n, 16, one, rest)

    def finish(k, carry):
        unfold(acc, M2, k, feat_ref)
        unfold(accw, MW, k, featw_ref)
        blk, out = target_chunk(k)
        x = [state[d, blk, :] - corner[d] for d in range(3)]
        v = [state[3 + d, blk, :] for d in range(3)]
        prs = pressure(state[6, blk, :])
        sym = [corr[r, blk, :] for r in range(6)]

        def total(ref, first_row, f):
            at = [ref[pl.ds((first_row + 3 * f + s) * 8, 8), :] for s in range(3)]
            return at[0] + (at[1] + at[2])

        shared = [total(feat_ref, 0, f) for f in range(13)]
        own = [total(feat_ref, W_ROWS, f) for f in range(29)]
        visc = [total(featw_ref, 0, f) for f in range(13)]
        m0, mx, mk, mkx = shared[0], shared[1:4], shared[4:10], shared[10:13]
        mv, mvx, mkv, mvkx = own[0:3], own[3:12], own[12:15], own[15]
        p0, px, pk, pkx = own[16], own[17:20], own[20:26], own[26:29]
        w0, wx, wk, wkx = visc[0], visc[1:4], visc[4:10], visc[10:13]
        vx = [[v[p] * (x[q] * m0 - mx[q]) - (mv[p] * x[q] - mvx[3 * p + q]) for q in range(3)] for p in range(3)]
        inner = jnp.zeros_like(m0)
        for p in range(3):
            for q in range(3):
                inner = inner + sym[SYM_INDEX[p][q]] * vx[p][q]
        mk_x = times(mk, x)
        for p in range(3):
            inner = inner + v[p] * (mk_x[p] - mkx[p]) - x[p] * mkv[p]
        inner = inner + mvkx
        live = state[7, blk, :] > 0.0
        rate[out, :] = jnp.where(live, (-0.5 * KERNEL_GRAD) * inner, 0.0)
        near = [prs * (x[p] * m0 - mx[p]) + (x[p] * p0 - px[p]) - 0.25 * (x[p] * w0 - wx[p]) for p in range(3)]
        mine = times(sym, near)
        pk_x = times(pk, x)
        wk_x = times(wk, x)
        for p in range(3):
            far = prs * (mk_x[p] - mkx[p]) + (pk_x[p] - pkx[p]) - 0.25 * (wk_x[p] - wkx[p])
            pull = -GRAVITY if p == 2 else 0.0
            accel[p, out, :] = jnp.where(live, (0.5 * KERNEL_GRAD) * (mine[p] + far) + pull, 0.0)
        return carry

    lax.fori_loop(0, 2 * levels, finish, 0)


VMEM = pl.BlockSpec(memory_space=pltpu.VMEM)
SMEM = pl.BlockSpec(memory_space=pltpu.SMEM)
ALL_COLUMNS = tuple((a, b) for a in range(1, 5) for b in range(1, 5))


def run_moments(table, strips):
    return pl.pallas_call(
        moment_kernel,
        out_shape=jax.ShapeDtypeStruct((6, LOCAL, 128), F32),
        in_specs=[SMEM] + [VMEM] * 6,
        out_specs=VMEM,
        scratch_shapes=[
            pltpu.VMEM((8, TOTAL, 128), F32),
            pltpu.VMEM((TOTAL, 128, KA), BF16),
            pltpu.VMEM((LOCAL, KA, 128), BF16),
            pltpu.VMEM((TOTAL, M1, 128), BF16),
            pltpu.VMEM((10 * 64, 128), F32),
            pltpu.VMEM((M1 * 8, 128), F32),
            pltpu.VMEM((4, NB * 128, 128), F32),
            pltpu.VMEM((LOCAL * M1, 128), F32),
        ],
        compiler_params=pltpu.CompilerParams(vmem_limit_bytes=56 * 2**20),
        name="moments",
    )(table, jnp.asarray(spread_matrix(), BF16), *strips)


def run_rates(table, strips, corr_strips):
    return pl.pallas_call(
        rate_kernel,
        out_shape=(jax.ShapeDtypeStruct((LOCAL, 128), F32), jax.ShapeDtypeStruct((3, LOCAL, 128), F32)),
        in_specs=[SMEM] + [VMEM] * 11,
        out_specs=(VMEM, VMEM),
        scratch_shapes=[
            pltpu.VMEM((8, TOTAL, 128), F32),
            pltpu.VMEM((6, TOTAL, 128), F32),
            pltpu.VMEM((TOTAL, 128, KA), BF16),
            pltpu.VMEM((LOCAL, KA, 256), BF16),
            pltpu.VMEM((TOTAL, 128, 128), F32),
            pltpu.VMEM((TOTAL, M2, 128), BF16),
            pltpu.VMEM((10 * 64, 128), F32),
            pltpu.VMEM((M2 * 8, 128), F32),
            pltpu.VMEM((MW * 8, 128), F32),
            pltpu.VMEM((4, NB * 128, 256), F32),
            pltpu.VMEM((LOCAL * M2, 128), F32),
            pltpu.VMEM((LOCAL * MW, 128), F32),
        ],
        compiler_params=pltpu.CompilerParams(vmem_limit_bytes=60 * 2**20),
        name="rates",
    )(table, jnp.asarray(spread_matrix(), BF16), *strips, *corr_strips)


def exchange(first, last, axis):
    count = lax.axis_size(axis)
    odd = lax.axis_index(axis) % 2 == 1
    inner = [(i, i ^ 1) for i in range(count)]
    outer = [(i, i + 1) for i in range(1, count - 1, 2)] + [(i + 1, i) for i in range(1, count - 1, 2)]
    across = lax.ppermute(jnp.where(odd, last, first), axis, outer)
    within = lax.ppermute(jnp.where(odd, first, last), axis, inner)
    return jnp.where(odd, within, across), jnp.where(odd, across, within)


def with_halo(blocks):
    low_y, high_y = exchange(blocks[:, :, :1], blocks[:, :, -1:], "gy")

    def row(a):
        return jnp.concatenate([low_y[:, a:a + 1], blocks[:, a:a + 1], high_y[:, a:a + 1]], 2)

    low_x, high_x = exchange(row(0), row(3), "gx")
    return [t.reshape(blocks.shape[0], -1, 128) for t in (blocks, low_y, high_y, low_x, high_x)]


def body(positions, velocity, density, masses, counts):
    shape = density.shape
    live = lax.broadcasted_iota(jnp.int32, shape, 3) < counts[..., None]
    mass = jnp.where(live, masses, 0.0)
    strips = with_halo(jnp.concatenate([positions, velocity, density[None], mass[None]], 0))
    table = jnp.asarray(item_table(ALL_COLUMNS))
    corr = run_moments(table, strips)
    corr_strips = with_halo(corr.reshape((6,) + shape))
    rate, accel = run_rates(table, strips, corr_strips)
    return (rate.reshape(shape), accel.reshape((3,) + shape))


def solution(mesh):
    return jax.shard_map(
        body,
        mesh=mesh,
        in_specs=(
            P(None, "gx", "gy", None, None),
            P(None, "gx", "gy", None, None),
            P("gx", "gy", None, None),
            P("gx", "gy", None, None),
            P("gx", "gy", None),
        ),
        out_specs=(P("gx", "gy", None, None), P(None, "gx", "gy", None, None)),
        check_vma=False,
    )
```
